128 devices in a mesh: fsdp: 16 (over z, x), tp: 8 (over y, core).
Axes of the slice: x: 4, y: 4, z: 4, core: 2. Of those that a mesh axis runs over, the one named last changes fastest.
Arguments:
- gradient: bfloat16 [8192, 14336], P('fsdp', 'tp'), may hold values from -6 to 6
- momentum: float32 [8192, 14336], P('fsdp', 'tp'), may hold values from -18 to 18
- basis: float32 [14336, 512], P('tp'), may hold values from -0.046875 to 0.046875
Outputs:
- new_momentum: float32 [8192, 14336], P('fsdp', 'tp')
- new_basis: float32 [14336, 512], P('tp')
- update: bfloat16 [8192, 14336], P('fsdp', 'tp')
The draws below stay inside these ranges and needn't reach their ends.
All inputs are finite; a program needn't handle non-finite values.
Results may differ from the reference program's by a relative error of at most 0.001.
Values sent between devices are 32-bit elements; how exact they have to be, the bound alone decides.
A program may use at most 128 MiB of HBM per device.

```python
import jax
import jax.numpy as jnp
from jax import lax

ROWS = 8192
COLS = 14336
RANK = 512


def block_levels(own_key, dims, shards, low, high):
    gain, own = 1.0, jax.random.fold_in(own_key, 6)
    for dim, parts in shards:
        heights = jnp.exp(jax.random.uniform(jax.random.fold_in(own, dim), (parts,), jnp.float32, low / len(shards), high / len(shards)))
        gain = gain * jnp.repeat(heights, dims[dim] // parts).reshape([-1 if axis == dim else 1 for axis in range(len(dims))])
    return gain


def gaussian(stream_key, extent, deviation, most, pieces=(), kind=jnp.bfloat16):
    values = deviation * jax.random.normal(stream_key, extent, jnp.float32)
    if pieces:
        values = values * block_levels(stream_key, extent, pieces, -0.22, 0.18)
    return jnp.clip(values, -most, most).astype(kind)


def setup_inputs(seed: int = 0) -> dict:
    key_list = jax.random.split(jax.random.key(seed), 4)
    return {
        "gradient": gaussian(key_list[0], (ROWS, COLS), 1.0, 6.0, ((0, 16), (1, 8))),
        "momentum": gaussian(key_list[1], (ROWS, COLS), 3.0, 18.0, ((0, 16), (1, 8)), jnp.float32),
        "basis": gaussian(key_list[2], (COLS, RANK), COLS ** -0.5, 0.046875, ((0, 8),), jnp.float32),
    }


def matmul(left, right):
    return jnp.dot(left.astype(jnp.float32), right.astype(jnp.float32), precision=lax.Precision.HIGHEST, preferred_element_type=jnp.float32)

def reference(gradient, momentum, basis):
    buffer = momentum + gradient.astype(jnp.float32)
    projected = matmul(buffer, basis)
    gram = matmul(projected.T, projected)
    lower = jnp.linalg.cholesky(gram)
    ortho = jax.scipy.linalg.solve_triangular(lower, projected.T, lower=True).T
    back = matmul(buffer.T, ortho)
    new_momentum = buffer - 0.05 * matmul(ortho, back.T)
    norms = jnp.sqrt(lax.optimization_barrier(jnp.sum(back * back, axis=0)))
    new_basis = back / (norms + 1e-08)
    scale = jnp.sqrt(jnp.float32(ROWS * COLS / RANK))
    update = (scale * matmul(ortho, new_basis.T)).astype(jnp.bfloat16)
    return (new_momentum, new_basis, update)
```

```python
import functools

import jax
import jax.numpy as jnp
from jax import lax
from jax.experimental import pallas as pl
from jax.experimental.pallas import tpu as pltpu
from jax.sharding import PartitionSpec as P

ROWS = 8192
COLS = 14336
RANK = 512
ROW = 512
COL = 1792
HALF = 256
CHUNK = 256
CHUNKS = COL // CHUNK
MESH = pl.DeviceIdType.MESH
HIGHEST = lax.Precision.HIGHEST
f32 = jnp.float32
bf16 = jnp.bfloat16


def split(value):
    high = value.astype(bf16)
    return high, (value - high.astype(f32)).astype(bf16)


def dot(left, right, dims=((1,), (0,)), precision=None):
    return lax.dot_general(left, right, (dims, ((), ())), precision=precision, preferred_element_type=f32)


def dot3(left, right, dims=((1,), (0,))):
    (lh, ll), (rh, rl) = left, right
    return dot(lh, rh, dims) + (dot(lh, rl, dims) + dot(ll, rh, dims))


def lanes(value, index):
    return jnp.take_along_axis(value, index, axis=1, mode="promise_in_bounds")


def factor128(tile, cols):
    sub = lax.broadcasted_iota(jnp.int32, (8, 128), 0)

    def row(ref, r, first):
        return jnp.broadcast_to(ref[r : r + 1, first : first + 128], (8, 128))

    for s in range(16):
        top = 8 * s
        block = tile[top : top + 8, 0:128]
        for j in range(8):
            cols[8 * j : 8 * j + 8, :] = lanes(block, jnp.full((8, 128), top + j, jnp.int32))
        d = {(i, j): row(cols, 8 * j + i, 0) for j in range(8) for i in range(j, 8)}
        ra = [row(tile, top + i, 0) for i in range(8)]
        re = [row(tile, top + i, 128) for i in range(8)]
        for j in range(8):
            inverse = lax.rsqrt(d[j, j])
            l = {i: d[i, j] * inverse for i in range(j + 1, 8)}
            for k in range(j + 1, 8):
                for i in range(k, 8):
                    d[i, k] = d[i, k] - l[i] * l[k]
            ra[j] = ra[j] * inverse
            re[j] = re[j] * inverse
            for i in range(j + 1, 8):
                ra[i] = ra[i] - l[i] * ra[j]
                re[i] = re[i] - l[i] * re[j]
        for i in range(8):
            tile[top + i : top + i + 1, 0:128] = ra[i][0:1]
            tile[top + i : top + i + 1, 128:256] = re[i][0:1]
        for t in range(s + 1, 16):
            at = slice(8 * t, 8 * t + 8)
            xa = tile[at, 0:128]
            xe = tile[at, 128:256]
            for k in range(8):
                c = lanes(ra[k], sub + 8 * t)
                xa = xa - c * ra[k]
                xe = xe - c * re[k]
            tile[at, 0:128] = xa
            tile[at, 128:256] = xe


def eye(n):
    return (lax.broadcasted_iota(jnp.int32, (n, n), 0) == lax.broadcasted_iota(jnp.int32, (n, n), 1)).astype(f32)


def factor_step(b, mat, tile, cols):
    n = 128
    lo, hi = b * n, b * n + n
    tile[:, 0:n] = mat[lo:hi, lo:hi]
    tile[:, n : 2 * n] = eye(n)
    factor128(tile, cols)
    mat[lo:hi, lo:hi] = eye(n)
    mat[lo:hi, :] = dot(tile[:, n : 2 * n], mat[lo:hi, :], precision=HIGHEST)
    if hi < RANK:
        mat[hi:, lo:hi] = jnp.zeros((RANK - hi, n), f32)
        mat[hi:, :] = mat[hi:, :] - dot(mat[lo:hi, hi:], mat[lo:hi, :], ((0,), (0,)), HIGHEST)


class Copies:
    def __init__(self, send, recv):
        self.send, self.recv, self.n, self.all = send, recv, 0, []

    def new(self, src, dst, device):
        i = self.n
        self.n += 1
        copy = pltpu.make_async_remote_copy(
            src_ref=src,
            dst_ref=dst,
            send_sem=self.send.at[i],
            recv_sem=self.recv.at[i],
            device_id=device,
            device_id_type=MESH,
        )
        copy.start()
        self.all.append(copy)
        return copy

    def finish(self):
        for copy in self.all:
            copy.wait_send()


class Ring:
    def __init__(self, copies, pos, right, left):
        self.copies, self.pos, self.right, self.left = copies, pos, right, left

    def at(self, base, size, step, half):
        offset = base + lax.rem(self.pos + step, 4) * size + half * (size // 2)
        return pl.ds(pl.multiple_of(offset, 8), size // 2)

    def reduce_start(self, ref, base, size, slots):
        new = self.copies.new
        self.ref, self.base, self.size, self.slots = ref, base, size, slots
        at = lambda step, half: ref.at[self.at(base, size, step, half)]
        self.r = [None] * 6
        self.r[0] = new(at(2, 0), slots.at[0], self.right)
        self.r[3] = new(at(2, 1), slots.at[3], self.left)

    def reduce_plain(self):
        new, ref, slots = self.copies.new, self.ref, self.slots
        at = lambda step, half: ref.at[self.at(self.base, self.size, step, half)]
        self.r[1] = new(at(1, 1), slots.at[1], self.right)
        self.r[4] = new(at(3, 0), slots.at[4], self.left)

    def reduce_middle(self):
        new, ref, slots = self.copies.new, self.ref, self.slots
        one = self.at(self.base, self.size, 1, 0)
        two = self.at(self.base, self.size, 3, 1)
        self.r[0].wait_recv()
        ref[one, :] = ref[one, :] + slots[0]
        self.r[2] = new(ref.at[one], slots.at[2], self.right)
        self.r[3].wait_recv()
        ref[two, :] = ref[two, :] + slots[3]
        self.r[5] = new(ref.at[two], slots.at[5], self.left)

    def reduce_end(self, out):
        ref, slots = self.ref, self.slots
        one = self.at(self.base, self.size, 0, 0)
        two = self.at(self.base, self.size, 0, 1)
        self.r[4].wait_recv()
        self.r[2].wait_recv()
        out[one, :] = ref[one, :] + slots[4] + slots[2]
        self.r[1].wait_recv()
        self.r[5].wait_recv()
        out[two, :] = ref[two, :] + slots[1] + slots[5]

    def gather_start(self, ref, base, size):
        new = self.copies.new
        self.gref, self.gbase, self.gsize = ref, base, size
        one = ref.at[self.at(base, size, 0, 0)]
        two = ref.at[self.at(base, size, 0, 1)]
        self.g = [None] * 6
        self.g[0] = new(one, one, self.right)
        self.g[2] = new(two, two, self.left)
        self.g[1] = new(two, two, self.right)
        self.g[3] = new(one, one, self.left)

    def gather_middle(self):
        new, ref = self.copies.new, self.gref
        one = ref.at[self.at(self.gbase, self.gsize, 3, 0)]
        two = ref.at[self.at(self.gbase, self.gsize, 1, 1)]
        self.g[0].wait_recv()
        self.g[4] = new(one, one, self.right)
        self.g[2].wait_recv()
        self.g[5] = new(two, two, self.left)

    def gather_end(self):
        for i in (1, 3, 4, 5):
            self.g[i].wait_recv()


def power_kernel(
    grad_hbm, mom_hbm, basis_hbm,
    w_ref, uh_ref, ul_ref, inv_ref,
    grad, mom, basis, bh, bl, qh, ql, bth, btl,
    pother, pown, precv, pslots, pfull, ph, plo,
    gpart, gslots, gmat, mat, tile, cols,
    zpart, zslots1, zslots2, zfull, lh, ll, squares, sqslots,
    load_sem, send_sem, recv_sem,
):
    f, t = lax.axis_index("fsdp"), lax.axis_index("tp")
    z, x, y, c = f // 4, f % 4, t // 2, t % 2

    def zdev(step):
        return (lax.rem(z + step, 4) * 4 + x, t)

    def xdev(step):
        return (z * 4 + lax.rem(x + step, 4), t)

    def ydev(step):
        return (f, lax.rem(y + step, 4) * 2 + c)

    def tdev(step):
        return (f, lax.rem(t + step, 8))

    sibling = (f, y * 2 + 1 - c)

    barrier = pltpu.get_barrier_semaphore()
    peers = [zdev(i) for i in (1, 2, 3)] + [xdev(i) for i in (1, 2, 3)] + [tdev(i) for i in range(1, 8)]
    for peer in peers:
        pl.semaphore_signal(barrier, inc=1, device_id=peer, device_id_type=MESH)

    loads = []
    for k in range(CHUNKS):
        at = pl.ds(k * CHUNK, CHUNK)
        loads.append([
            pltpu.make_async_copy(mom_hbm.at[:, at], mom.at[:, at], load_sem.at[3 * k]),
            pltpu.make_async_copy(grad_hbm.at[:, at], grad.at[:, at], load_sem.at[3 * k + 1]),
            pltpu.make_async_copy(basis_hbm.at[at, :], basis.at[at, :], load_sem.at[3 * k + 2]),
        ])
        for load in loads[-1]:
            load.start()

    copies = Copies(send_sem, recv_sem)

    def partial(k, half):
        at = slice(k * CHUNK, k * CHUNK + CHUNK)
        columns = pl.ds(pl.multiple_of(half * HALF, HALF), HALF)
        return dot3((bh[:, at], bl[:, at]), (qh[at, columns], ql[at, columns]))

    for k in range(CHUNKS):
        at = slice(k * CHUNK, k * CHUNK + CHUNK)
        for load in loads[k]:
            load.wait()
        bh[:, at], bl[:, at] = split(mom[:, at] + grad[:, at].astype(f32))
        qh[at, :], ql[at, :] = split(basis[at, :])
        term = partial(k, 1 - c)
        pother[...] = term if k == 0 else pother[...] + term

    pl.semaphore_wait(barrier, len(peers))
    swap = copies.new(pother, precv, sibling)
    for k in range(CHUNKS):
        term = partial(k, c)
        pown[...] = term if k == 0 else pown[...] + term
    swap.wait_recv()
    pown[...] = pown[...] + precv[...]

    def transposed(k):
        at = slice(k * CHUNK, k * CHUNK + CHUNK)
        bth[at, :], btl[at, :] = split((mom[:, at] + grad[:, at].astype(f32)).T)

    yring = Ring(copies, y, ydev(1), ydev(3))
    yring.reduce_start(pown, 0, 128, pslots)
    yring.reduce_plain()
    for k in (0, 1):
        transposed(k)
    yring.reduce_middle()
    for k in (2, 3):
        transposed(k)
    mine = pfull.at[c]
    yring.reduce_end(mine)
    yring.gather_start(mine, 0, 128)
    group = lambda step: mine.at[pl.ds(pl.multiple_of(lax.rem(y + step, 4) * 128, 128), 128)]
    shared = [copies.new(group(0), group(0), sibling)]
    for k in (4, 5):
        transposed(k)
    yring.gather_middle()
    transposed(6)
    yring.gather_end()
    for step in (1, 2, 3):
        shared.append(copies.new(group(step), group(step), sibling))
    ph[c], plo[c] = split(pfull[c])
    for copy in shared:
        copy.wait_recv()
    ph[1 - c], plo[1 - c] = split(pfull[1 - c])

    gat = pl.ds(pl.multiple_of((y % 2) * 128, 128), 128)
    gl = (ph[y // 2, :, gat], plo[y // 2, :, gat])
    for half in range(2):
        g = dot3(gl, (ph[half], plo[half]), ((0,), (0,)))
        gpart[0, :, half * HALF : half * HALF + HALF] = jnp.where(c == 0, g[0:32], g[64:96])
        gpart[1, :, half * HALF : half * HALF + HALF] = jnp.where(c == 0, g[32:64], g[96:128])

    def gram_send(stage):
        first, second = (zdev, xdev) if stage == 0 else (xdev, zdev)
        sent = []
        for step in (1, 2, 3):
            sent.append(copies.new(gpart.at[2 * stage], gslots.at[stage, 0, step - 1], first(step)))
            sent.append(copies.new(gpart.at[2 * stage + 1], gslots.at[stage, 1, step - 1], second(step)))
        return sent

    def gram_sum(stage, sent):
        for copy in sent:
            copy.wait_recv()
        for part in range(2):
            own = gpart[2 * stage + part]
            total = own + gslots[stage, part, 0] + gslots[stage, part, 1] + gslots[stage, part, 2]
            if stage == 0:
                gpart[2 + part] = total
            else:
                gmat[pl.ds(pl.multiple_of(t * 64 + part * 32, 32), 32), :] = total

    sent = gram_send(0)

    zring = Ring(copies, z, zdev(1), zdev(3))
    xring = Ring(copies, x, xdev(1), xdev(3))
    rings = ((zring, xring), (xring, zring))
    first = [Ring(copies, z, zdev(1), zdev(3)), Ring(copies, x, xdev(1), xdev(3))]
    second = [Ring(copies, x, xdev(1), xdev(3)), Ring(copies, z, zdev(1), zdev(3))]
    tall = COL // 4
    short = tall // 4
    bases = [z * tall, x * tall]

    def product(half, step):
        rows = tall // 2
        start = lax.rem(first[half].pos + step, 4) * tall

        @pl.loop(0, 2)
        def _(i):
            at = pl.ds(pl.multiple_of(start + i * rows, 32), rows)
            zpart[half, at, :] = dot3((bth[at, :], btl[at, :]), (ph[half], plo[half]))

    for half in range(2):
        product(half, 2)
        first[half].reduce_start(zpart.at[half], 0, tall, zslots1.at[half])
    for half in range(2):
        product(half, 1)
        product(half, 3)
        first[half].reduce_plain()
    gram_sum(0, sent)
    sent = gram_send(1)
    for half in range(2):
        product(half, 0)
    gram_sum(1, sent)
    rows64 = lambda step: gmat.at[pl.ds(pl.multiple_of((lax.rem(y + step, 4) * 2 + c) * 64, 64), 64)]
    spread = [copies.new(rows64(0), rows64(0), ydev(i)) for i in (1, 2, 3)]
    shared = [copies.new(rows64(0), rows64(0), sibling)]
    for half in range(2):
        first[half].reduce_middle()
    for i in (1, 2, 3):
        spread[i - 1].wait_recv()
        shared.append(copies.new(rows64(4 - i), rows64(4 - i), sibling))
    for copy in shared:
        copy.wait_recv()

    mat[...] = gmat[...]
    factor_step(0, mat, tile, cols)
    for half in range(2):
        first[half].reduce_end(zpart.at[half])
        second[half].reduce_start(zpart.at[half], bases[half], short, zslots2.at[half])
        second[half].reduce_plain()
    factor_step(1, mat, tile, cols)
    for half in range(2):
        second[half].reduce_middle()
    for half in range(2):
        second[half].reduce_end(zfull.at[half])
        second[half].gather_start(zfull.at[half], bases[half], short)
    factor_step(2, mat, tile, cols)
    for half in range(2):
        second[half].gather_middle()
    for half in range(2):
        second[half].gather_end()
        first[half].gather_start(zfull.at[half], 0, tall)
    factor_step(3, mat, tile, cols)
    r = lax.broadcasted_iota(jnp.int32, (RANK, RANK), 0)
    k = lax.broadcasted_iota(jnp.int32, (RANK, RANK), 1)
    lh[...], ll[...] = split(jnp.where(r >= k, mat[...], 0.0))
    uh_ref[...], ul_ref[...] = split(
        sum(
            dot3((ph[half], plo[half]), (lh[:, half * HALF : half * HALF + HALF], ll[:, half * HALF : half * HALF + HALF]), ((1,), (1,)))
            for half in range(2)
        )
    )
    for half in range(2):
        first[half].gather_middle()
    for half in range(2):
        first[half].gather_end()

    squares[0] = jnp.zeros((8, RANK), f32)

    @pl.loop(0, CHUNKS)
    def _(i):
        at = pl.ds(pl.multiple_of(i * CHUNK, CHUNK), CHUNK)
        w = sum(
            dot3(split(zfull[half, at, :]), (lh[:, half * HALF : half * HALF + HALF], ll[:, half * HALF : half * HALF + HALF]), ((1,), (1,)))
            for half in range(2)
        )
        w_ref[at, :] = w
        squares[0] = squares[0] + jnp.sum((w * w).reshape(CHUNK // 8, 8, RANK), axis=0)

    sent = [copies.new(squares.at[0], sqslots.at[i - 1], tdev(i)) for i in range(1, 8)]
    total = squares[0]
    for i in range(7):
        sent[i].wait_recv()
        total = total + sqslots[i]
    norms = jnp.sqrt(jnp.sum(total, axis=0, keepdims=True))
    inv_ref[...] = jnp.broadcast_to(1.0 / (norms + 1e-08), (8, RANK))
    copies.finish()


COPIES = 128


def power(gradient, momentum, basis):
    vmem = lambda shape, kind=f32: pltpu.VMEM(shape, kind)
    any_spec = pl.BlockSpec(memory_space=pl.ANY)
    vmem_spec = pl.BlockSpec(memory_space=pltpu.VMEM)
    return pl.pallas_call(
        power_kernel,
        out_shape=[
            jax.ShapeDtypeStruct((COL, RANK), f32),
            jax.ShapeDtypeStruct((ROW, RANK), bf16),
            jax.ShapeDtypeStruct((ROW, RANK), bf16),
            jax.ShapeDtypeStruct((8, RANK), f32),
        ],
        in_specs=[any_spec] * 3,
        out_specs=[vmem_spec] * 4,
        scratch_shapes=[
            vmem((ROW, COL), bf16), vmem((ROW, COL)), vmem((COL, RANK)),
            vmem((ROW, COL), bf16), vmem((ROW, COL), bf16),
            vmem((COL, RANK), bf16), vmem((COL, RANK), bf16),
            vmem((COL, ROW), bf16), vmem((COL, ROW), bf16),
            vmem((ROW, HALF)), vmem((ROW, HALF)), vmem((ROW, HALF)),
            vmem((6, 64, HALF)), vmem((2, ROW, HALF)),
            vmem((2, ROW, HALF), bf16), vmem((2, ROW, HALF), bf16),
            vmem((4, 32, RANK)), vmem((2, 2, 3, 32, RANK)), vmem((RANK, RANK)), vmem((RANK, RANK)),
            vmem((128, 256)), vmem((64, 128)),
            vmem((2, COL, HALF)), vmem((2, 6, COL // 8, HALF)), vmem((2, 6, COL // 32, HALF)),
            vmem((2, COL, HALF)),
            vmem((RANK, RANK), bf16), vmem((RANK, RANK), bf16),
            vmem((1, 8, RANK)), vmem((7, 8, RANK)),
            pltpu.SemaphoreType.DMA((3 * CHUNKS,)),
            pltpu.SemaphoreType.DMA((COPIES,)),
            pltpu.SemaphoreType.DMA((COPIES,)),
        ],
        compiler_params=pltpu.CompilerParams(
            collective_id=0, has_side_effects=True, vmem_limit_bytes=60 << 20
        ),
        name="power",
    )(gradient, momentum, basis)


def apply_kernel(scale, w_ref, uh, ul, inv, mom, grad, nm_ref, nb_ref, up_ref):
    w = w_ref[...]
    nb = w * inv[0:1, :]
    nb_ref[...] = nb
    high, low = split(nb)
    u = uh[...]
    last = ((1,), (1,))
    up_ref[...] = (scale * dot3((u, ul[...]), (high, low), last)).astype(bf16)
    nm_ref[...] = (mom[...] + grad[...].astype(f32)) - 0.05 * dot(u, w.astype(bf16), last)


def apply(w, uh, ul, inv, momentum, gradient):
    scale = float((ROWS * COLS / RANK) ** 0.5)
    whole = lambda shape: pl.BlockSpec(shape, lambda i: (0, 0))
    across = pl.BlockSpec((ROW, CHUNK), lambda i: (0, i))
    down = pl.BlockSpec((CHUNK, RANK), lambda i: (i, 0))
    return pl.pallas_call(
        functools.partial(apply_kernel, scale),
        grid=(CHUNKS,),
        out_shape=[
            jax.ShapeDtypeStruct((ROW, COL), f32),
            jax.ShapeDtypeStruct((COL, RANK), f32),
            jax.ShapeDtypeStruct((ROW, COL), bf16),
        ],
        in_specs=[down, whole((ROW, RANK)), whole((ROW, RANK)), whole((8, RANK)), across, across],
        out_specs=[across, down, across],
        compiler_params=pltpu.CompilerParams(vmem_limit_bytes=60 << 20),
        name="apply",
    )(w, uh, ul, inv, momentum, gradient)


def local(gradient, momentum, basis):
    w, uh, ul, inv = power(gradient, momentum, basis)
    return tuple(apply(w, uh, ul, inv, momentum, gradient))


def solution(mesh):
    return jax.shard_map(
        local,
        mesh=mesh,
        in_specs=(P("fsdp", "tp"), P("fsdp", "tp"), P("tp", None)),
        out_specs=(P("fsdp", "tp"), P("tp", None), P("fsdp", "tp")),
        check_vma=False,
    )
```

```python
import functools

import jax
import jax.numpy as jnp
from jax import lax
from jax.experimental import pallas as pl
from jax.experimental.pallas import tpu as pltpu
from jax.sharding import PartitionSpec as P

ROWS = 8192
COLS = 14336
RANK = 512
ROW = 512
COL = 1792
HALF = 256
CHUNK = 256
CHUNKS = COL // CHUNK
MESH = pl.DeviceIdType.MESH
HIGHEST = lax.Precision.HIGHEST
f32 = jnp.float32
bf16 = jnp.bfloat16


def split(value):
    high = value.astype(bf16)
    return high, (value - high.astype(f32)).astype(bf16)


def dot(left, right, dims=((1,), (0,)), precision=None):
    return lax.dot_general(left, right, (dims, ((), ())), precision=precision, preferred_element_type=f32)


def dot3(left, right, dims=((1,), (0,))):
    (lh, ll), (rh, rl) = left, right
    return dot(lh, rh, dims) + (dot(lh, rl, dims) + dot(ll, rh, dims))


def lanes(value, index):
    return jnp.take_along_axis(value, index, axis=1, mode="promise_in_bounds")


def factor128(tile, cols, steps):
    sub = lax.broadcasted_iota(jnp.int32, (8, 128), 0)

    def row(ref, r, first):
        return jnp.broadcast_to(ref[r : r + 1, first : first + 128], (8, 128))

    for s in steps:
        top = 8 * s
        block = tile[top : top + 8, 0:128]
        for j in range(8):
            cols[8 * j : 8 * j + 8, :] = lanes(block, jnp.full((8, 128), top + j, jnp.int32))
        d = {(i, j): row(cols, 8 * j + i, 0) for j in range(8) for i in range(j, 8)}
        ra = [row(tile, top + i, 0) for i in range(8)]
        re = [row(tile, top + i, 128) for i in range(8)]
        for j in range(8):
            inverse = lax.rsqrt(d[j, j])
            l = {i: d[i, j] * inverse for i in range(j + 1, 8)}
            for k in range(j + 1, 8):
                for i in range(k, 8):
                    d[i, k] = d[i, k] - l[i] * l[k]
            ra[j] = ra[j] * inverse
            re[j] = re[j] * inverse
            for i in range(j + 1, 8):
                ra[i] = ra[i] - l[i] * ra[j]
                re[i] = re[i] - l[i] * re[j]
        for i in range(8):
            tile[top + i : top + i + 1, 0:128] = ra[i][0:1]
            tile[top + i : top + i + 1, 128:256] = re[i][0:1]
        for t in range(s + 1, 16):
            at = slice(8 * t, 8 * t + 8)
            xa = tile[at, 0:128]
            xe = tile[at, 128:256]
            for k in range(8):
                c = lanes(ra[k], sub + 8 * t)
                xa = xa - c * ra[k]
                xe = xe - c * re[k]
            tile[at, 0:128] = xa
            tile[at, 128:256] = xe


def eye(n):
    return (lax.broadcasted_iota(jnp.int32, (n, n), 0) == lax.broadcasted_iota(jnp.int32, (n, n), 1)).astype(f32)


def factor(mat, tile, cols):
    n = 128
    for lo in range(0, RANK, n):
        hi = lo + n
        tile[:, 0:n] = mat[lo:hi, lo:hi]
        tile[:, n : 2 * n] = eye(n)
        for part in range(4):
            factor128(tile, cols, range(4 * part, 4 * part + 4))
            yield
        mat[lo:hi, lo:hi] = eye(n)
        mat[lo:hi, :] = dot(tile[:, n : 2 * n], mat[lo:hi, :], precision=HIGHEST)
        if hi < RANK:
            mat[hi:, lo:hi] = jnp.zeros((RANK - hi, n), f32)
            mat[hi:, :] = mat[hi:, :] - dot(mat[lo:hi, hi:], mat[lo:hi, :], ((0,), (0,)), HIGHEST)
        yield


class Copies:
    def __init__(self, send, recv):
        self.send, self.recv = send, recv
        self.free, self.fresh, self.n, self.all, self.drained = [], 0, 0, [], 0

    def semaphore(self):
        self.n += 1
        return self.recv.at[self.n - 1]

    def new(self, src, dst, device, recv=None):
        if self.free:
            i = self.free.pop(0)
        else:
            i = self.fresh
            self.fresh += 1
        copy = pltpu.make_async_remote_copy(
            src_ref=src,
            dst_ref=dst,
            send_sem=self.send.at[i],
            recv_sem=self.semaphore() if recv is None else recv,
            device_id=device,
            device_id_type=MESH,
        )
        copy.start()
        self.all.append((copy, i))
        return copy

    def drain(self, upto):
        for copy, i in self.all[self.drained : upto]:
            copy.wait_send()
            self.free.append(i)
        self.drained = upto

    def count(self):
        return len(self.all)


def arrive(ref, semaphore):
    pltpu.make_async_copy(ref, ref, semaphore).wait()


class Ring:
    def __init__(self, copies, pos, right, left):
        self.copies, self.pos, self.right, self.left = copies, pos, right, left

    def place(self, base, size):
        first = (size // 2 + 7) // 8 * 8

        def at(step, part):
            offset = base + lax.rem(self.pos + step, 4) * size + part * first
            return pl.ds(pl.multiple_of(offset, 8), size - first if part else first)

        return at

    def reduce_start(self, ref, base, size, slots):
        new = self.copies.new
        at = self.place(base, size)
        self.ref, self.at = ref, at
        self.slots = [slots.at[i, 0 : at(0, 1 if i in (1, 3, 5) else 0).size] for i in range(6)]
        self.r = [None] * 6
        self.rest, self.whole = self.copies.semaphore(), slots.at[0:4]
        self.r[0] = new(ref.at[at(2, 0)], self.slots[0], self.right)
        self.r[3] = new(ref.at[at(2, 1)], self.slots[3], self.left)

    def reduce_plain(self):
        new, ref, at = self.copies.new, self.ref, self.at
        self.r[1] = new(ref.at[at(1, 1)], self.slots[1], self.right, self.rest)
        self.r[4] = new(ref.at[at(3, 0)], self.slots[4], self.left, self.rest)

    def reduce_middle(self):
        new, ref, slots = self.copies.new, self.ref, self.slots
        one, two = self.at(1, 0), self.at(3, 1)
        self.r[0].wait_recv()
        ref[one, :] = ref[one, :] + slots[0][...]
        self.r[2] = new(ref.at[one], slots[2], self.right, self.rest)
        self.r[3].wait_recv()
        ref[two, :] = ref[two, :] + slots[3][...]
        self.r[5] = new(ref.at[two], slots[5], self.left, self.rest)

    def reduce_end(self, out):
        ref, slots = self.ref, self.slots
        one, two = self.at(0, 0), self.at(0, 1)
        arrive(self.whole, self.rest)
        out[one, :] = ref[one, :] + slots[4][...] + slots[2][...]
        out[two, :] = ref[two, :] + slots[1][...] + slots[5][...]

    def gather_start(self, ref, base, size):
        new = self.copies.new
        at = self.place(base, size)
        self.out, self.gat = ref, at
        one, two = ref.at[at(0, 0)], ref.at[at(0, 1)]
        self.g = [None] * 6
        self.grest, self.gwhole = self.copies.semaphore(), ref.at[pl.ds(base, 2 * size)]
        self.g[0] = new(one, one, self.right)
        self.g[2] = new(two, two, self.left)
        self.g[1] = new(two, two, self.right, self.grest)
        self.g[3] = new(one, one, self.left, self.grest)

    def gather_middle(self):
        new, ref, at = self.copies.new, self.out, self.gat
        one, two = ref.at[at(3, 0)], ref.at[at(1, 1)]
        self.g[0].wait_recv()
        self.g[4] = new(one, one, self.right, self.grest)
        self.g[2].wait_recv()
        self.g[5] = new(two, two, self.left, self.grest)

    def gather_end(self):
        arrive(self.gwhole, self.grest)


class Direct:
    def __init__(self, copies, pos, dev):
        self.copies, self.pos, self.dev = copies, pos, dev

    def group(self, step):
        return pl.ds(pl.multiple_of(self.base + lax.rem(self.pos + step, 4) * self.size, 8), self.size)

    def reduce_start(self, ref, base, size, slots):
        self.ref, self.base, self.size, self.slots = ref, base, size, slots
        self.sem = self.copies.semaphore()
        for i in (2, 1, 3):
            self.copies.new(ref.at[self.group(i)], slots.at[i - 1], self.dev(i), self.sem)

    def reduce_end(self, out):
        arrive(self.slots, self.sem)
        at = self.group(0)
        out[at, :] = (self.ref[at, :] + self.slots[0]) + (self.slots[1] + self.slots[2])

    def gather_start(self, ref):
        own = ref.at[self.group(0)]
        self.sem = self.copies.semaphore()
        for i in (2, 1, 3):
            self.copies.new(own, own, self.dev(i), self.sem)

    def gather_end(self):
        arrive(self.slots, self.sem)


def dion_kernel(
    grad_hbm, mom_hbm, basis_hbm,
    nm_ref, nb_ref, uh, ul, inv_ref,
    grad, mom, bh, bl, qh, ql,
    pacc, pother, pown, precv, pslots, pfull, ph, plo,
    prow, gpart, gsum, gslots1, gslots2, gslots3, gmat, mat, tile, cols,
    zpart, zslots1, zslots2, zfull, lh, ll, squares, sqslots,
    load_sem, send_sem, recv_sem,
):
    f, t = lax.axis_index("fsdp"), lax.axis_index("tp")
    z, x, y, c = f // 4, f % 4, t // 2, t % 2

    def zdev(step):
        return (lax.rem(z + step, 4) * 4 + x, t)

    def xdev(step):
        return (z * 4 + lax.rem(x + step, 4), t)

    def ydev(step):
        return (f, lax.rem(y + step, 4) * 2 + c)

    def tdev(step):
        return (f, lax.rem(t + step, 8))

    sibling = (f, y * 2 + 1 - c)

    barrier = pltpu.get_barrier_semaphore()
    peers = [zdev(i) for i in (1, 2, 3)] + [xdev(i) for i in (1, 2, 3)] + [tdev(i) for i in range(1, 8)]
    for peer in peers:
        pl.semaphore_signal(barrier, inc=1, device_id=peer, device_id_type=MESH)

    def load(k):
        at = pl.ds(k * CHUNK, CHUNK)
        pltpu.make_async_copy(mom_hbm.at[:, at], mom.at[:, at], load_sem.at[k]).start()
        pltpu.make_async_copy(grad_hbm.at[:, at], grad.at[:, at], load_sem.at[k]).start()
        for half in range(2):
            pltpu.make_async_copy(
                basis_hbm.at[at, pl.ds(half * HALF, HALF)], zfull.at[half, at], load_sem.at[k]
            ).start()

    for k in range(CHUNKS):
        load(k)
    loaded = zpart.at[0, 0:1280]

    copies = Copies(send_sem, recv_sem)

    def partial(q, k):
        at = slice(k * CHUNK, k * CHUNK + CHUNK)
        columns = slice(q * HALF, q * HALF + HALF)
        term = dot3((bh[:, at], bl[:, at]), (qh[at, columns], ql[at, columns]))
        pacc[q] = term if k == 0 else pacc[q] + term

    def swap_start(q):
        pother[q] = pacc[q, :, pl.ds(pl.multiple_of((1 - c) * 128, 128), 128)]
        return copies.new(pother.at[q], precv.at[q], sibling)

    yring = [Ring(copies, y, ydev(1), ydev(3)) for _ in range(2)]

    def yrs_start(q):
        swaps[q].wait_recv()
        pown[q] = pacc[q, :, pl.ds(pl.multiple_of(c * 128, 128), 128)] + precv[q]
        yring[q].reduce_start(pown.at[q], 0, 128, pslots.at[q])
        yring[q].reduce_plain()

    shared = [[copies.semaphore() for _ in range(2)] for _ in range(2)]

    def share(q, step, semaphore):
        part = pfull.at[q, c, pl.ds(pl.multiple_of(lax.rem(y + step, 4) * 128, 128), 128)]
        copies.new(part, part, sibling, semaphore)

    def yrs_end(q):
        yring[q].reduce_end(pfull.at[q, c])
        yring[q].gather_start(pfull.at[q, c], 0, 128)
        share(q, 0, shared[q][0])

    def yag_end(q):
        yring[q].gather_end()
        for step in (1, 2, 3):
            share(q, step, shared[q][1])

    for k in range(CHUNKS):
        at = slice(k * CHUNK, k * CHUNK + CHUNK)
        arrive(loaded, load_sem.at[k])
        bh[:, at], bl[:, at] = split(mom[:, at] + grad[:, at].astype(f32))
        for half in range(2):
            columns = slice(half * HALF, half * HALF + HALF)
            qh[at, columns], ql[at, columns] = split(zfull[half, at, :])
        partial(0, k)
    pl.semaphore_wait(barrier, len(peers))
    swaps = [swap_start(0)]
    for k in range(CHUNKS):
        partial(1, k)
    swaps.append(swap_start(1))
    yrs_start(0)
    yrs_start(1)
    yring[0].reduce_middle()
    yring[1].reduce_middle()
    yrs_end(0)
    yrs_end(1)

    own_rows = pl.ds(pl.multiple_of(y * 128, 128), 128)
    for q in range(2):
        arrive(precv.at[q, 0:128], shared[q][0])
        for j in range(2):
            prow[:, q * HALF + j * 128 : q * HALF + j * 128 + 128] = pfull[q, j, own_rows, :]
    block = lambda i, width=1: prow[:, pl.ds(pl.multiple_of(i * 128, 128), width * 128)]
    over = ((0,), (0,))
    gpart[:, 0:384] = dot(block(c), block(c, 3), over, HIGHEST)
    gpart[:, 384:512] = dot(block(2 * c), block(3 - c), over, HIGHEST)
    gpart[:, 512:640] = dot(block(3 - c), block(3), over, HIGHEST)
    parts = (pl.ds(0, 384), pl.ds(384, 256))
    axes = ((z, zdev), (x, xdev))

    def rows(pos, step, size, base=0):
        return pl.ds(pl.multiple_of(base + lax.rem(pos + step, 4) * size, 8), size)

    def gram_send(stage):
        semaphore = copies.semaphore()
        for step in (1, 2, 3):
            for g in range(2):
                (pos, dev), (pos2, dev2) = axes[g], axes[1 - g]
                if stage == 1:
                    src, dst, to = gpart.at[rows(pos, step, 32), parts[g]], gslots1.at[step - 1, :, parts[g]], dev(step)
                elif stage == 2:
                    at = rows(pos2, step, 8, pos * 32)
                    src, dst, to = gsum.at[at, parts[g]], gslots2.at[step - 1, :, parts[g]], dev2(step)
                elif stage == 3:
                    at = rows(pos2, 0, 8, pos * 32)
                    src, dst, to = gsum.at[at, parts[g]], gslots3.at[step - 1, :, parts[g]], ydev(step)
                elif stage == 4:
                    at = rows(pos2, 0, 8, pos * 32)
                    src, dst, to = gmat.at[c, at, parts[g]], gmat.at[c, at, parts[g]], dev2(step)
                else:
                    at = rows(pos, 0, 32)
                    src, dst, to = gmat.at[c, at, parts[g]], gmat.at[c, at, parts[g]], dev(step)
                copies.new(src, dst, to, semaphore)
        return semaphore

    def gram_wait(stage, sent):
        arrive({1: gslots1, 2: gslots2, 3: gslots3, 4: gslots3, 5: gslots1}[stage], sent)
        if stage > 3:
            return
        for g in range(2):
            pos, pos2 = axes[g][0], axes[1 - g][0]
            if stage == 1:
                at = rows(pos, 0, 32)
                own, slots, out = gpart[at, parts[g]], gslots1, gsum
            elif stage == 2:
                at = rows(pos2, 0, 8, pos * 32)
                own, slots, out = gsum[at, parts[g]], gslots2, gsum
            else:
                at = rows(pos2, 0, 8, pos * 32)
                own, slots, out = gsum[at, parts[g]], gslots3, gmat.at[c]
            out[at, parts[g]] = (own + slots[0, :, parts[g]]) + (slots[1, :, parts[g]] + slots[2, :, parts[g]])

    sent = gram_send(1)
    yring[0].gather_middle()
    yring[1].gather_middle()
    yag_end(0)

    def product(q):
        arrive(precv.at[q, 0:384], shared[q][1])
        for j in range(2):
            ph[q, :, j * 128 : j * 128 + 128], plo[q, :, j * 128 : j * 128 + 128] = split(pfull[q, j])
        for k in range(CHUNKS):
            at = slice(k * CHUNK, k * CHUNK + CHUNK)
            zpart[q, at, :] = dot3((bh[:, at], bl[:, at]), (ph[q], plo[q]), ((0,), (0,)))

    tall = COL // 8
    short = tall // 4
    starts = (0, COL // 2)
    bases = (z * tall, COL // 2 + x * tall)
    first = [[Ring(copies, z, zdev(1), zdev(3)), Ring(copies, x, xdev(1), xdev(3))] for _ in range(2)]
    second = [[Direct(copies, x, xdev), Direct(copies, z, zdev)] for _ in range(2)]

    def rs1_start(q):
        for g in range(2):
            first[q][g].reduce_start(zpart.at[q], starts[g], tall, zslots1.at[q, g])
        for g in range(2):
            first[q][g].reduce_plain()

    def rs1_middle(q):
        for g in range(2):
            first[q][g].reduce_middle()

    def rs1_end(q):
        for g in range(2):
            first[q][g].reduce_end(zpart.at[q])
            second[q][g].reduce_start(zpart.at[q], bases[g], short, zslots2.at[q, g])

    def rs2_end(q):
        for g in range(2):
            second[q][g].reduce_end(zfull.at[q])
            second[q][g].gather_start(zfull.at[q])

    def ag1_end(q):
        for g in range(2):
            second[q][g].gather_end()
            first[q][g].gather_start(zfull.at[q], starts[g], tall)

    def ag2_middle(q):
        for g in range(2):
            first[q][g].gather_middle()

    def ag2_end(q):
        for g in range(2):
            first[q][g].gather_end()

    gram_wait(1, sent)
    sent = gram_send(2)
    product(0)
    gram_wait(2, sent)
    sent = gram_send(3)
    rs1_start(0)
    sums_sent = copies.count()
    yag_end(1)
    product(1)
    copies.drain(sums_sent - 20)
    gram_wait(3, sent)
    sent = gram_send(4)
    rs1_middle(0)
    gram_wait(4, sent)
    sent = gram_send(5)
    rs1_start(1)
    first_sent = copies.count()
    rs1_end(0)
    gram_wait(5, sent)
    swap = copies.new(gmat.at[c], gmat.at[c], sibling)
    rs1_middle(1)
    swap.wait_recv()
    for i, g, first_block, width, where in (
        (0, 0, 0, 3, 0), (0, 0, 3, 1, 384), (3, 0, 3, 1, 512),
        (1, 1, 1, 3, 0), (2, 1, 2, 1, 384), (2, 1, 3, 1, 512),
    ):
        mat[i * 128 : i * 128 + 128, first_block * 128 : (first_block + width) * 128] = gmat[
            g, :, where : where + width * 128
        ]

    work = factor(mat, tile, cols)

    def steps(n):
        for _ in range(n):
            next(work)

    steps(1)
    rs2_end(0)
    steps(2)
    rs1_end(1)
    steps(2)
    ag1_end(0)
    copies.drain(first_sent)
    steps(3)
    rs2_end(1)
    steps(3)
    ag2_middle(0)
    ag1_end(1)
    most_sent = copies.count() - 16
    steps(6)
    ag2_middle(1)
    steps(3)
    r = lax.broadcasted_iota(jnp.int32, (RANK, RANK), 0)
    k = lax.broadcasted_iota(jnp.int32, (RANK, RANK), 1)
    lh[...], ll[...] = split(jnp.where(r >= k, mat[...], 0.0))
    last = ((1,), (1,))

    def solve(pairs):
        low, high = slice(0, HALF), slice(HALF, RANK)
        factor_of = lambda rows_, columns: (lh[rows_, columns], ll[rows_, columns])
        left = dot3(pairs[0], factor_of(low, low), last)
        right = dot3(pairs[0], factor_of(high, low), last) + dot3(pairs[1], factor_of(high, high), last)
        return left, right

    shard = [
        jnp.concatenate([zfull[q, second[q][g].group(0), :] for g in range(2)], axis=0) for q in range(2)
    ]
    for q, w in enumerate(solve([split(part) for part in shard])):
        squares[0, :, q * HALF : q * HALF + HALF] = jnp.sum((w * w).reshape(short // 4, 8, HALF), axis=0)

    def norm_send(stage):
        steps_, dev = ((1, 2, 3), zdev) if stage == 0 else ((1, 2, 3), xdev) if stage == 1 else (range(1, 8), tdev)
        semaphore = copies.semaphore()
        for i in steps_:
            copies.new(squares.at[stage], sqslots.at[stage, i - 1], dev(i), semaphore)
        return semaphore

    def norm_wait(stage, sent):
        total = squares[stage]
        number = 7 if stage == 2 else 3
        arrive(sqslots.at[stage, 0:number], sent)
        for i in range(number):
            total = total + sqslots[stage, i]
        squares[stage + 1] = total

    sent = norm_send(0)
    for q, u in enumerate(solve([(ph[half], plo[half]) for half in range(2)])):
        at = slice(q * HALF, q * HALF + HALF)
        uh[:, at], ul[:, at] = split(u)

    low, high = slice(0, HALF), slice(HALF, RANK)

    def early(k):
        at = slice(k * CHUNK, k * CHUNK + CHUNK)
        part = split(zfull[0, at, :])
        nb_ref[at, low] = dot3(part, (lh[low, low], ll[low, low]), last)
        nb_ref[at, high] = dot3(part, (lh[high, low], ll[high, low]), last)

    def back(k):
        at = slice(k * CHUNK, k * CHUNK + CHUNK)
        nb_ref[at, high] = nb_ref[at, high] + dot3(split(zfull[1, at, :]), (lh[high, high], ll[high, high]), last)
        update = dot(uh[...], nb_ref[at, :].astype(bf16), last)
        nm_ref[:, at] = (mom[:, at] + grad[:, at].astype(f32)) - 0.05 * update

    ag2_end(0)
    norm_wait(0, sent)
    sent = norm_send(1)
    for i in range(4):
        early(i)
    norm_wait(1, sent)
    sent = norm_send(2)
    for i in range(4, CHUNKS):
        early(i)
    copies.drain(most_sent)
    ag2_end(1)
    for i in range(CHUNKS):
        back(i)
    norm_wait(2, sent)
    norms = jnp.sqrt(jnp.sum(squares[3], axis=0, keepdims=True))
    inv_ref[...] = jnp.broadcast_to(1.0 / (norms + 1e-08), (8, RANK))
    copies.drain(copies.count())


def finish_kernel(scale, nm, w, uh, ul, inv, nm_out, nb_out, up_out, nb, up, sem):
    pltpu.make_async_copy(nm, nm_out, sem.at[0]).start()
    for k in range(CHUNKS):
        at = slice(k * CHUNK, k * CHUNK + CHUNK)
        n = w[at, :] * inv[0:1, :]
        nb[at, :] = n
        pltpu.make_async_copy(nb.at[at, :], nb_out.at[at, :], sem.at[1]).start()
        up[:, at] = (scale * dot3((uh[...], ul[...]), split(n), ((1,), (1,)))).astype(bf16)
        pltpu.make_async_copy(up.at[:, at], up_out.at[:, at], sem.at[2]).start()
    for i, (src, dst) in enumerate(((nm, nm_out), (nb, nb_out), (up, up_out))):
        pltpu.make_async_copy(src, dst, sem.at[i]).wait()


SENDS = 78
ARRIVALS = 59


def local(gradient, momentum, basis):
    vmem = lambda shape, kind=f32: pltpu.VMEM(shape, kind)
    shapes = [
        jax.ShapeDtypeStruct((ROW, COL), f32),
        jax.ShapeDtypeStruct((COL, RANK), f32),
        jax.ShapeDtypeStruct((ROW, COL), bf16),
    ]
    results = pl.pallas_call(
        dion_kernel,
        out_shape=shapes[:2] + [
            jax.ShapeDtypeStruct((ROW, RANK), bf16),
            jax.ShapeDtypeStruct((ROW, RANK), bf16),
            jax.ShapeDtypeStruct((8, RANK), f32),
        ],
        in_specs=[pl.BlockSpec(memory_space=pltpu.HBM)] * 3,
        out_specs=[pl.BlockSpec(memory_space=pltpu.VMEM)] * 5,
        scratch_shapes=[
            vmem((ROW, COL), bf16), vmem((ROW, COL)),
            vmem((ROW, COL), bf16), vmem((ROW, COL), bf16),
            vmem((COL, RANK), bf16), vmem((COL, RANK), bf16),
            vmem((2, ROW, HALF)), vmem((2, ROW, 128)), vmem((2, ROW, 128)), vmem((2, ROW, 128)),
            vmem((2, 6, 64, 128)), vmem((2, 2, ROW, 128)),
            vmem((2, ROW, HALF), bf16), vmem((2, ROW, HALF), bf16),
            vmem((128, RANK)), vmem((128, 640)), vmem((128, 640)),
            vmem((3, 32, 640)), vmem((3, 8, 640)), vmem((3, 8, 640)), vmem((2, 128, 640)), vmem((RANK, RANK)),
            vmem((128, 256)), vmem((64, 128)),
            vmem((2, COL, HALF)), vmem((2, 2, 6, COL // 16, HALF)), vmem((2, 2, 3, COL // 32, HALF)),
            vmem((2, COL, HALF)),
            vmem((RANK, RANK), bf16), vmem((RANK, RANK), bf16),
            vmem((4, 8, RANK)), vmem((3, 7, 8, RANK)),
            pltpu.SemaphoreType.DMA((CHUNKS,)),
            pltpu.SemaphoreType.DMA((SENDS,)),
            pltpu.SemaphoreType.DMA((ARRIVALS,)),
        ],
        compiler_params=pltpu.CompilerParams(
            collective_id=0, has_side_effects=True, vmem_limit_bytes=40 << 20
        ),
        name="dion",
    )(*(pltpu.with_memory_space_constraint(a, pltpu.HBM) for a in (gradient, momentum, basis)))
    return tuple(pl.pallas_call(
        functools.partial(finish_kernel, float((ROWS * COLS / RANK) ** 0.5)),
        out_shape=shapes,
        in_specs=[pl.BlockSpec(memory_space=pltpu.VMEM)] * 5,
        out_specs=[pl.BlockSpec(memory_space=pltpu.HBM)] * 3,
        scratch_shapes=[vmem((COL, RANK)), vmem((ROW, COL), bf16), pltpu.SemaphoreType.DMA((3,))],
        compiler_params=pltpu.CompilerParams(vmem_limit_bytes=10 << 20),
        name="finish",
    )(*results))


def solution(mesh):
    return jax.shard_map(
        local,
        mesh=mesh,
        in_specs=(P("fsdp", "tp"), P("fsdp", "tp"), P("tp", None)),
        out_specs=(P("fsdp", "tp"), P("tp", None), P("fsdp", "tp")),
        check_vma=False,
    )
```

```python
import functools

import jax
import jax.numpy as jnp
from jax import lax
from jax.experimental import pallas as pl
from jax.experimental.pallas import tpu as pltpu
from jax.sharding import PartitionSpec as P

ROWS = 8192
COLS = 14336
RANK = 512
ROW = 512
COL = 1792
HALF = 256
CHUNK = 256
CHUNKS = COL // CHUNK
MESH = pl.DeviceIdType.MESH
HIGHEST = lax.Precision.HIGHEST
f32 = jnp.float32
bf16 = jnp.bfloat16


def split(value):
    high = value.astype(bf16)
    return high, (value - high.astype(f32)).astype(bf16)


def dot(left, right, dims=((1,), (0,)), precision=None):
    return lax.dot_general(left, right, (dims, ((), ())), precision=precision, preferred_element_type=f32)


def dot3(left, right, dims=((1,), (0,))):
    (lh, ll), (rh, rl) = left, right
    return dot(lh, rh, dims) + (dot(lh, rl, dims) + dot(ll, rh, dims))


def lanes(value, index):
    return jnp.take_along_axis(value, index, axis=1, mode="promise_in_bounds")


def factor128(tile, cols, steps):
    sub = lax.broadcasted_iota(jnp.int32, (8, 128), 0)

    def row(ref, r, first):
        return jnp.broadcast_to(ref[r : r + 1, first : first + 128], (8, 128))

    for s in steps:
        top = 8 * s
        block = tile[top : top + 8, 0:128]
        for j in range(8):
            cols[8 * j : 8 * j + 8, :] = lanes(block, jnp.full((8, 128), top + j, jnp.int32))
        d = {(i, j): row(cols, 8 * j + i, 0) for j in range(8) for i in range(j, 8)}
        ra = [row(tile, top + i, 0) for i in range(8)]
        re = [row(tile, top + i, 128) for i in range(8)]
        for j in range(8):
            inverse = lax.rsqrt(d[j, j])
            l = {i: d[i, j] * inverse for i in range(j + 1, 8)}
            for k in range(j + 1, 8):
                for i in range(k, 8):
                    d[i, k] = d[i, k] - l[i] * l[k]
            ra[j] = ra[j] * inverse
            re[j] = re[j] * inverse
            for i in range(j + 1, 8):
                ra[i] = ra[i] - l[i] * ra[j]
                re[i] = re[i] - l[i] * re[j]
        for i in range(8):
            tile[top + i : top + i + 1, 0:128] = ra[i][0:1]
            tile[top + i : top + i + 1, 128:256] = re[i][0:1]
        for t in range(s + 1, 16):
            at = slice(8 * t, 8 * t + 8)
            xa = tile[at, 0:128]
            xe = tile[at, 128:256]
            for k in range(8):
                c = lanes(ra[k], sub + 8 * t)
                xa = xa - c * ra[k]
                xe = xe - c * re[k]
            tile[at, 0:128] = xa
            tile[at, 128:256] = xe


def eye(n):
    return (lax.broadcasted_iota(jnp.int32, (n, n), 0) == lax.broadcasted_iota(jnp.int32, (n, n), 1)).astype(f32)


def factor(mat, tile, cols):
    n = 128
    for lo in range(0, RANK, n):
        hi = lo + n
        tile[:, 0:n] = mat[lo:hi, lo:hi]
        tile[:, n : 2 * n] = eye(n)
        for part in range(4):
            factor128(tile, cols, range(4 * part, 4 * part + 4))
            yield
        mat[lo:hi, lo:hi] = eye(n)
        mat[lo:hi, :] = dot(tile[:, n : 2 * n], mat[lo:hi, :], precision=HIGHEST)
        if hi < RANK:
            mat[hi:, lo:hi] = jnp.zeros((RANK - hi, n), f32)
            mat[hi:, :] = mat[hi:, :] - dot(mat[lo:hi, hi:], mat[lo:hi, :], ((0,), (0,)), HIGHEST)
        yield


class Copies:
    def __init__(self, send, recv):
        self.send, self.recv = send, recv
        self.free, self.fresh, self.n, self.all, self.drained = [], 0, 0, [], 0

    def semaphore(self):
        self.n += 1
        return self.recv.at[self.n - 1]

    def new(self, src, dst, device, recv=None):
        if self.free:
            i = self.free.pop(0)
        else:
            i = self.fresh
            self.fresh += 1
        copy = pltpu.make_async_remote_copy(
            src_ref=src,
            dst_ref=dst,
            send_sem=self.send.at[i],
            recv_sem=self.semaphore() if recv is None else recv,
            device_id=device,
            device_id_type=MESH,
        )
        copy.start()
        self.all.append((copy, i))
        return copy

    def drain(self, upto):
        for copy, i in self.all[self.drained : upto]:
            copy.wait_send()
            self.free.append(i)
        self.drained = upto

    def count(self):
        return len(self.all)


def arrive(ref, semaphore):
    pltpu.make_async_copy(ref, ref, semaphore).wait()


class Ring:
    def __init__(self, copies, pos, right, left):
        self.copies, self.pos, self.right, self.left = copies, pos, right, left

    def place(self, base, size):
        first = (size // 2 + 7) // 8 * 8

        def at(step, part):
            offset = base + lax.rem(self.pos + step, 4) * size + part * first
            return pl.ds(pl.multiple_of(offset, 8), size - first if part else first)

        return at

    def reduce_start(self, ref, base, size, slots):
        new = self.copies.new
        at = self.place(base, size)
        self.ref, self.at = ref, at
        self.slots = [slots.at[i, 0 : at(0, 1 if i in (1, 3, 5) else 0).size] for i in range(6)]
        self.r = [None] * 6
        self.rest, self.whole = self.copies.semaphore(), slots.at[0:4]
        self.r[0] = new(ref.at[at(2, 0)], self.slots[0], self.right)
        self.r[3] = new(ref.at[at(2, 1)], self.slots[3], self.left)

    def reduce_plain(self):
        new, ref, at = self.copies.new, self.ref, self.at
        self.r[1] = new(ref.at[at(1, 1)], self.slots[1], self.right, self.rest)
        self.r[4] = new(ref.at[at(3, 0)], self.slots[4], self.left, self.rest)

    def reduce_middle(self):
        new, ref, slots = self.copies.new, self.ref, self.slots
        one, two = self.at(1, 0), self.at(3, 1)
        self.r[0].wait_recv()
        ref[one, :] = ref[one, :] + slots[0][...]
        self.r[2] = new(ref.at[one], slots[2], self.right, self.rest)
        self.r[3].wait_recv()
        ref[two, :] = ref[two, :] + slots[3][...]
        self.r[5] = new(ref.at[two], slots[5], self.left, self.rest)

    def reduce_end(self, out):
        ref, slots = self.ref, self.slots
        one, two = self.at(0, 0), self.at(0, 1)
        arrive(self.whole, self.rest)
        out[one, :] = ref[one, :] + slots[4][...] + slots[2][...]
        out[two, :] = ref[two, :] + slots[1][...] + slots[5][...]

    def gather_start(self, ref, base, size):
        new = self.copies.new
        at = self.place(base, size)
        self.out, self.gat = ref, at
        one, two = ref.at[at(0, 0)], ref.at[at(0, 1)]
        self.g = [None] * 6
        self.grest, self.gwhole = self.copies.semaphore(), ref.at[pl.ds(base, 2 * size)]
        self.g[0] = new(one, one, self.right)
        self.g[2] = new(two, two, self.left)

    def gather_rest(self):
        new, ref, at = self.copies.new, self.out, self.gat
        one, two = ref.at[at(0, 0)], ref.at[at(0, 1)]
        self.g[1] = new(two, two, self.right, self.grest)
        self.g[3] = new(one, one, self.left, self.grest)

    def gather_middle(self):
        new, ref, at = self.copies.new, self.out, self.gat
        one, two = ref.at[at(3, 0)], ref.at[at(1, 1)]
        self.g[0].wait_recv()
        self.g[4] = new(one, one, self.right, self.grest)
        self.g[2].wait_recv()
        self.g[5] = new(two, two, self.left, self.grest)

    def gather_end(self):
        arrive(self.gwhole, self.grest)


class Direct:
    def __init__(self, copies, pos, dev):
        self.copies, self.pos, self.dev = copies, pos, dev

    def group(self, step):
        return pl.ds(pl.multiple_of(self.base + lax.rem(self.pos + step, 4) * self.size, 8), self.size)

    def reduce_start(self, ref, base, size, slots):
        self.ref, self.base, self.size, self.slots = ref, base, size, slots
        self.sem = self.copies.semaphore()
        for i in (2, 1, 3):
            self.copies.new(ref.at[self.group(i)], slots.at[i - 1], self.dev(i), self.sem)

    def reduce_end(self, out):
        arrive(self.slots, self.sem)
        at = self.group(0)
        out[at, :] = (self.ref[at, :] + self.slots[0]) + (self.slots[1] + self.slots[2])

    def gather_start(self, ref):
        own = ref.at[self.group(0)]
        self.sem = self.copies.semaphore()
        for i in (2, 1, 3):
            self.copies.new(own, own, self.dev(i), self.sem)

    def gather_end(self):
        arrive(self.slots, self.sem)


def dion_kernel(
    grad_hbm, mom_hbm, basis_hbm,
    nm_ref, nb_ref, uh, ul, inv_ref,
    grad, mom, bh, bl, qh, ql,
    pacc, pother, pown, precv, pslots, pfull, ph, plo,
    prow, gpart, gsum, gslots1, gslots2, gslots3, gmat, mat, tile, cols,
    zpart, zslots1, zslots2, zfull, lh, ll, squares, sqslots,
    load_sem, send_sem, recv_sem,
):
    f, t = lax.axis_index("fsdp"), lax.axis_index("tp")
    z, x, y, c = f // 4, f % 4, t // 2, t % 2

    def zdev(step):
        return (lax.rem(z + step, 4) * 4 + x, t)

    def xdev(step):
        return (z * 4 + lax.rem(x + step, 4), t)

    def ydev(step):
        return (f, lax.rem(y + step, 4) * 2 + c)

    def tdev(step):
        return (f, lax.rem(t + step, 8))

    sibling = (f, y * 2 + 1 - c)

    barrier = pltpu.get_barrier_semaphore()
    peers = [zdev(i) for i in (1, 2, 3)] + [xdev(i) for i in (1, 2, 3)] + [tdev(i) for i in range(1, 8)]
    for peer in peers:
        pl.semaphore_signal(barrier, inc=1, device_id=peer, device_id_type=MESH)

    def load(k):
        at = pl.ds(k * CHUNK, CHUNK)
        pltpu.make_async_copy(mom_hbm.at[:, at], mom.at[:, at], load_sem.at[k]).start()
        pltpu.make_async_copy(grad_hbm.at[:, at], grad.at[:, at], load_sem.at[k]).start()
        for half in range(2):
            pltpu.make_async_copy(
                basis_hbm.at[at, pl.ds(half * HALF, HALF)], zfull.at[half, at], load_sem.at[k]
            ).start()

    for k in range(CHUNKS):
        load(k)
    loaded = zpart.at[0, 0:1280]

    copies = Copies(send_sem, recv_sem)

    def partial(q, k):
        at = slice(k * CHUNK, k * CHUNK + CHUNK)
        columns = slice(q * HALF, q * HALF + HALF)
        term = dot3((bh[:, at], bl[:, at]), (qh[at, columns], ql[at, columns]))
        pacc[q] = term if k == 0 else pacc[q] + term

    def swap_start(q):
        pother[q] = pacc[q, :, pl.ds(pl.multiple_of((1 - c) * 128, 128), 128)]
        return copies.new(pother.at[q], precv.at[q], sibling)

    yring = [Ring(copies, y, ydev(1), ydev(3)) for _ in range(2)]

    def yrs_start(q):
        swaps[q].wait_recv()
        pown[q] = pacc[q, :, pl.ds(pl.multiple_of(c * 128, 128), 128)] + precv[q]
        yring[q].reduce_start(pown.at[q], 0, 128, pslots.at[q])
        yring[q].reduce_plain()

    shared = [[copies.semaphore() for _ in range(2)] for _ in range(2)]

    def share(q, step, semaphore):
        part = pfull.at[q, c, pl.ds(pl.multiple_of(lax.rem(y + step, 4) * 128, 128), 128)]
        copies.new(part, part, sibling, semaphore)

    def yrs_end(q):
        yring[q].reduce_end(pfull.at[q, c])
        yring[q].gather_start(pfull.at[q, c], 0, 128)
        yring[q].gather_rest()
        share(q, 0, shared[q][0])

    def yag_end(q):
        yring[q].gather_end()
        for step in (1, 2, 3):
            share(q, step, shared[q][1])

    for k in range(CHUNKS):
        at = slice(k * CHUNK, k * CHUNK + CHUNK)
        arrive(loaded, load_sem.at[k])
        bh[:, at], bl[:, at] = split(mom[:, at] + grad[:, at].astype(f32))
        for half in range(2):
            columns = slice(half * HALF, half * HALF + HALF)
            qh[at, columns], ql[at, columns] = split(zfull[half, at, :])
        partial(0, k)
    pl.semaphore_wait(barrier, len(peers))
    swaps = [swap_start(0)]
    for k in range(CHUNKS):
        partial(1, k)
    swaps.append(swap_start(1))
    yrs_start(0)
    yrs_start(1)
    yring[0].reduce_middle()
    yring[1].reduce_middle()
    yrs_end(0)
    yrs_end(1)

    own_rows = pl.ds(pl.multiple_of(y * 128, 128), 128)
    for q in range(2):
        arrive(precv.at[q, 0:128], shared[q][0])
        for j in range(2):
            prow[:, q * HALF + j * 128 : q * HALF + j * 128 + 128] = pfull[q, j, own_rows, :]
    block = lambda i, width=1: prow[:, pl.ds(pl.multiple_of(i * 128, 128), width * 128)]
    over = ((0,), (0,))
    gpart[:, 0:384] = dot(block(c), block(c, 3), over, HIGHEST)
    gpart[:, 384:512] = dot(block(2 * c), block(3 - c), over, HIGHEST)
    gpart[:, 512:640] = dot(block(3 - c), block(3), over, HIGHEST)
    parts = (pl.ds(0, 384), pl.ds(384, 256))
    axes = ((z, zdev), (x, xdev))

    def rows(pos, step, size, base=0):
        return pl.ds(pl.multiple_of(base + lax.rem(pos + step, 4) * size, 8), size)

    def gram_send(stage):
        semaphore = copies.semaphore()
        for step in (1, 2, 3):
            for g in range(2):
                (pos, dev), (pos2, dev2) = axes[g], axes[1 - g]
                if stage == 1:
                    src, dst, to = gpart.at[rows(pos, step, 32), parts[g]], gslots1.at[step - 1, :, parts[g]], dev(step)
                elif stage == 2:
                    at = rows(pos2, step, 8, pos * 32)
                    src, dst, to = gsum.at[at, parts[g]], gslots2.at[step - 1, :, parts[g]], dev2(step)
                elif stage == 3:
                    at = rows(pos2, 0, 8, pos * 32)
                    src, dst, to = gsum.at[at, parts[g]], gslots3.at[step - 1, :, parts[g]], ydev(step)
                elif stage == 4:
                    at = rows(pos2, 0, 8, pos * 32)
                    src, dst, to = gmat.at[c, at, parts[g]], gmat.at[c, at, parts[g]], dev2(step)
                else:
                    at = rows(pos, 0, 32)
                    src, dst, to = gmat.at[c, at, parts[g]], gmat.at[c, at, parts[g]], dev(step)
                copies.new(src, dst, to, semaphore)
        return semaphore

    def gram_wait(stage, sent):
        arrive({1: gslots1, 2: gslots2, 3: gslots3, 4: gslots3, 5: gslots1}[stage], sent)
        if stage > 3:
            return
        for g in range(2):
            pos, pos2 = axes[g][0], axes[1 - g][0]
            if stage == 1:
                at = rows(pos, 0, 32)
                own, slots, out = gpart[at, parts[g]], gslots1, gsum
            elif stage == 2:
                at = rows(pos2, 0, 8, pos * 32)
                own, slots, out = gsum[at, parts[g]], gslots2, gsum
            else:
                at = rows(pos2, 0, 8, pos * 32)
                own, slots, out = gsum[at, parts[g]], gslots3, gmat.at[c]
            out[at, parts[g]] = (own + slots[0, :, parts[g]]) + (slots[1, :, parts[g]] + slots[2, :, parts[g]])

    sent = gram_send(1)
    yring[0].gather_middle()
    yring[1].gather_middle()
    yag_end(0)

    def product(q):
        arrive(precv.at[q, 0:384], shared[q][1])
        for j in range(2):
            ph[q, :, j * 128 : j * 128 + 128], plo[q, :, j * 128 : j * 128 + 128] = split(pfull[q, j])
        for k in range(CHUNKS):
            at = slice(k * CHUNK, k * CHUNK + CHUNK)
            zpart[q, at, :] = dot3((bh[:, at], bl[:, at]), (ph[q], plo[q]), ((0,), (0,)))

    tall = COL // 8
    short = tall // 4
    starts = (0, COL // 2)
    bases = (z * tall, COL // 2 + x * tall)
    first = [[Ring(copies, z, zdev(1), zdev(3)), Ring(copies, x, xdev(1), xdev(3))] for _ in range(2)]
    second = [[Direct(copies, x, xdev), Direct(copies, z, zdev)] for _ in range(2)]

    def rs1_start(q):
        for g in range(2):
            first[q][g].reduce_start(zpart.at[q], starts[g], tall, zslots1.at[q, g])
        for g in range(2):
            first[q][g].reduce_plain()

    def rs1_middle(q):
        for g in range(2):
            first[q][g].reduce_middle()

    def rs1_end(q):
        for g in range(2):
            first[q][g].reduce_end(zpart.at[q])
            second[q][g].reduce_start(zpart.at[q], bases[g], short, zslots2.at[q, g])

    def rs2_end(q):
        for g in range(2):
            second[q][g].reduce_end(zfull.at[q])
            second[q][g].gather_start(zfull.at[q])

    def ag1_end(q):
        for g in range(2):
            second[q][g].gather_end()
            first[q][g].gather_start(zfull.at[q], starts[g], tall)

    def ag2_rest(q):
        for g in range(2):
            first[q][g].gather_rest()

    def ag2_middle(q):
        for g in range(2):
            first[q][g].gather_middle()

    def ag2_end(q):
        for g in range(2):
            first[q][g].gather_end()

    gram_wait(1, sent)
    sent = gram_send(2)
    product(0)
    gram_wait(2, sent)
    sent = gram_send(3)
    rs1_start(0)
    sums_sent = copies.count()
    yag_end(1)
    product(1)
    copies.drain(sums_sent - 20)
    gram_wait(3, sent)
    sent = gram_send(4)
    rs1_middle(0)
    gram_wait(4, sent)
    sent = gram_send(5)
    rs1_start(1)
    first_sent = copies.count()
    rs1_end(0)
    gram_wait(5, sent)
    swap = copies.new(gmat.at[c], gmat.at[c], sibling)
    swap.wait_recv()
    for i, g, first_block, width, where in (
        (0, 0, 0, 3, 0), (0, 0, 3, 1, 384), (3, 0, 3, 1, 512),
        (1, 1, 1, 3, 0), (2, 1, 2, 1, 384), (2, 1, 3, 1, 512),
    ):
        mat[i * 128 : i * 128 + 128, first_block * 128 : (first_block + width) * 128] = gmat[
            g, :, where : where + width * 128
        ]

    work = factor(mat, tile, cols)

    def steps(n):
        for _ in range(n):
            next(work)

    steps(2)
    rs1_middle(1)
    steps(4)
    rs2_end(0)
    steps(3)
    rs1_end(1)
    steps(2)
    ag1_end(0)
    steps(3)
    rs2_end(1)
    ag2_rest(0)
    copies.drain(first_sent)
    steps(4)
    ag2_middle(0)
    steps(2)
    r = lax.broadcasted_iota(jnp.int32, (RANK, RANK), 0)
    k = lax.broadcasted_iota(jnp.int32, (RANK, RANK), 1)
    lh[...], ll[...] = split(jnp.where(r >= k, mat[...], 0.0))
    last = ((1,), (1,))

    def solve(pairs):
        low, high = slice(0, HALF), slice(HALF, RANK)
        factor_of = lambda rows_, columns: (lh[rows_, columns], ll[rows_, columns])
        left = dot3(pairs[0], factor_of(low, low), last)
        right = dot3(pairs[0], factor_of(high, low), last) + dot3(pairs[1], factor_of(high, high), last)
        return left, right

    shard = [
        jnp.concatenate([zfull[q, second[q][g].group(0), :] for g in range(2)], axis=0) for q in range(2)
    ]
    for q, w in enumerate(solve([split(part) for part in shard])):
        squares[0, :, q * HALF : q * HALF + HALF] = jnp.sum((w * w).reshape(short // 4, 8, HALF), axis=0)

    def norm_send(stage):
        steps_, dev = ((1, 2, 3), zdev) if stage == 0 else ((1, 2, 3), xdev) if stage == 1 else (range(1, 8), tdev)
        semaphore = copies.semaphore()
        for i in steps_:
            copies.new(squares.at[stage], sqslots.at[stage, i - 1], dev(i), semaphore)
        return semaphore

    def norm_wait(stage, sent):
        total = squares[stage]
        number = 7 if stage == 2 else 3
        arrive(sqslots.at[stage, 0:number], sent)
        for i in range(number):
            total = total + sqslots[stage, i]
        squares[stage + 1] = total

    sent = norm_send(0)
    ag1_end(1)
    for q, u in enumerate(solve([(ph[half], plo[half]) for half in range(2)])):
        at = slice(q * HALF, q * HALF + HALF)
        uh[:, at], ul[:, at] = split(u)

    low, high = slice(0, HALF), slice(HALF, RANK)

    def early(k):
        at = slice(k * CHUNK, k * CHUNK + CHUNK)
        part = split(zfull[0, at, :])
        nb_ref[at, low] = dot3(part, (lh[low, low], ll[low, low]), last)
        nb_ref[at, high] = dot3(part, (lh[high, low], ll[high, low]), last)

    def back(k):
        at = slice(k * CHUNK, k * CHUNK + CHUNK)
        nb_ref[at, high] = nb_ref[at, high] + dot3(split(zfull[1, at, :]), (lh[high, high], ll[high, high]), last)
        update = dot(uh[...], nb_ref[at, :].astype(bf16), last)
        nm_ref[:, at] = (mom[:, at] + grad[:, at].astype(f32)) - 0.05 * update

    ag2_rest(1)
    most_sent = copies.count() - 16
    norm_wait(0, sent)
    sent = norm_send(1)
    ag2_end(0)
    for i in range(3):
        early(i)
    ag2_middle(1)
    norm_wait(1, sent)
    sent = norm_send(2)
    for i in range(3, CHUNKS):
        early(i)
    copies.drain(most_sent)
    ag2_end(1)
    for i in range(CHUNKS):
        back(i)
    norm_wait(2, sent)
    norms = jnp.sqrt(jnp.sum(squares[3], axis=0, keepdims=True))
    inv_ref[...] = jnp.broadcast_to(1.0 / (norms + 1e-08), (8, RANK))
    copies.drain(copies.count())


def finish_kernel(scale, nm, w, uh, ul, inv, nm_out, nb_out, up_out, nb, up, sem):
    pltpu.make_async_copy(nm, nm_out, sem.at[0]).start()
    for k in range(CHUNKS):
        at = slice(k * CHUNK, k * CHUNK + CHUNK)
        n = w[at, :] * inv[0:1, :]
        nb[at, :] = n
        pltpu.make_async_copy(nb.at[at, :], nb_out.at[at, :], sem.at[1]).start()
        up[:, at] = (scale * dot3((uh[...], ul[...]), split(n), ((1,), (1,)))).astype(bf16)
        pltpu.make_async_copy(up.at[:, at], up_out.at[:, at], sem.at[2]).start()
    for i, (src, dst) in enumerate(((nm, nm_out), (nb, nb_out), (up, up_out))):
        pltpu.make_async_copy(src, dst, sem.at[i]).wait()


SENDS = 84
ARRIVALS = 59


def local(gradient, momentum, basis):
    vmem = lambda shape, kind=f32: pltpu.VMEM(shape, kind)
    shapes = [
        jax.ShapeDtypeStruct((ROW, COL), f32),
        jax.ShapeDtypeStruct((COL, RANK), f32),
        jax.ShapeDtypeStruct((ROW, COL), bf16),
    ]
    results = pl.pallas_call(
        dion_kernel,
        out_shape=shapes[:2] + [
            jax.ShapeDtypeStruct((ROW, RANK), bf16),
            jax.ShapeDtypeStruct((ROW, RANK), bf16),
            jax.ShapeDtypeStruct((8, RANK), f32),
        ],
        in_specs=[pl.BlockSpec(memory_space=pltpu.HBM)] * 3,
        out_specs=[pl.BlockSpec(memory_space=pltpu.VMEM)] * 5,
        scratch_shapes=[
            vmem((ROW, COL), bf16), vmem((ROW, COL)),
            vmem((ROW, COL), bf16), vmem((ROW, COL), bf16),
            vmem((COL, RANK), bf16), vmem((COL, RANK), bf16),
            vmem((2, ROW, HALF)), vmem((2, ROW, 128)), vmem((2, ROW, 128)), vmem((2, ROW, 128)),
            vmem((2, 6, 64, 128)), vmem((2, 2, ROW, 128)),
            vmem((2, ROW, HALF), bf16), vmem((2, ROW, HALF), bf16),
            vmem((128, RANK)), vmem((128, 640)), vmem((128, 640)),
            vmem((3, 32, 640)), vmem((3, 8, 640)), vmem((3, 8, 640)), vmem((2, 128, 640)), vmem((RANK, RANK)),
            vmem((128, 256)), vmem((64, 128)),
            vmem((2, COL, HALF)), vmem((2, 2, 6, COL // 16, HALF)), vmem((2, 2, 3, COL // 32, HALF)),
            vmem((2, COL, HALF)),
            vmem((RANK, RANK), bf16), vmem((RANK, RANK), bf16),
            vmem((4, 8, RANK)), vmem((3, 7, 8, RANK)),
            pltpu.SemaphoreType.DMA((CHUNKS,)),
            pltpu.SemaphoreType.DMA((SENDS,)),
            pltpu.SemaphoreType.DMA((ARRIVALS,)),
        ],
        compiler_params=pltpu.CompilerParams(
            collective_id=0, has_side_effects=True, vmem_limit_bytes=40 << 20
        ),
        name="dion",
    )(*(pltpu.with_memory_space_constraint(a, pltpu.HBM) for a in (gradient, momentum, basis)))
    return tuple(pl.pallas_call(
        functools.partial(finish_kernel, float((ROWS * COLS / RANK) ** 0.5)),
        out_shape=shapes,
        in_specs=[pl.BlockSpec(memory_space=pltpu.VMEM)] * 5,
        out_specs=[pl.BlockSpec(memory_space=pltpu.HBM)] * 3,
        scratch_shapes=[vmem((COL, RANK)), vmem((ROW, COL), bf16), pltpu.SemaphoreType.DMA((3,))],
        compiler_params=pltpu.CompilerParams(vmem_limit_bytes=10 << 20),
        name="finish",
    )(*results))


def solution(mesh):
    return jax.shard_map(
        local,
        mesh=mesh,
        in_specs=(P("fsdp", "tp"), P("fsdp", "tp"), P("tp", None)),
        out_specs=(P("fsdp", "tp"), P("tp", None), P("fsdp", "tp")),
        check_vma=False,
    )
```

```python
import functools

import jax
import jax.numpy as jnp
from jax import lax
from jax.experimental import pallas as pl
from jax.experimental.pallas import tpu as pltpu
from jax.sharding import PartitionSpec as P

ROWS = 8192
COLS = 14336
RANK = 512
ROW = 512
COL = 1792
HALF = 256
CHUNK = 256
CHUNKS = COL // CHUNK
MESH = pl.DeviceIdType.MESH
HIGHEST = lax.Precision.HIGHEST
f32 = jnp.float32
bf16 = jnp.bfloat16


def split(value):
    high = value.astype(bf16)
    return high, (value - high.astype(f32)).astype(bf16)


def dot(left, right, dims=((1,), (0,)), precision=None):
    return lax.dot_general(left, right, (dims, ((), ())), precision=precision, preferred_element_type=f32)


def dot3(left, right, dims=((1,), (0,))):
    (lh, ll), (rh, rl) = left, right
    return dot(lh, rh, dims) + (dot(lh, rl, dims) + dot(ll, rh, dims))


def lanes(value, index):
    return jnp.take_along_axis(value, index, axis=1, mode="promise_in_bounds")


def factor128(tile, cols, steps):
    sub = lax.broadcasted_iota(jnp.int32, (8, 128), 0)

    def row(ref, r, first):
        return jnp.broadcast_to(ref[r : r + 1, first : first + 128], (8, 128))

    for s in steps:
        top = 8 * s
        block = tile[top : top + 8, 0:128]
        for j in range(8):
            cols[8 * j : 8 * j + 8, :] = lanes(block, jnp.full((8, 128), top + j, jnp.int32))
        d = {(i, j): row(cols, 8 * j + i, 0) for j in range(8) for i in range(j, 8)}
        ra = [row(tile, top + i, 0) for i in range(8)]
        re = [row(tile, top + i, 128) for i in range(8)]
        for j in range(8):
            inverse = lax.rsqrt(d[j, j])
            l = {i: d[i, j] * inverse for i in range(j + 1, 8)}
            for k in range(j + 1, 8):
                for i in range(k, 8):
                    d[i, k] = d[i, k] - l[i] * l[k]
            ra[j] = ra[j] * inverse
            re[j] = re[j] * inverse
            for i in range(j + 1, 8):
                ra[i] = ra[i] - l[i] * ra[j]
                re[i] = re[i] - l[i] * re[j]
        for i in range(8):
            tile[top + i : top + i + 1, 0:128] = ra[i][0:1]
            tile[top + i : top + i + 1, 128:256] = re[i][0:1]
        for t in range(s + 1, 16):
            at = slice(8 * t, 8 * t + 8)
            xa = tile[at, 0:128]
            xe = tile[at, 128:256]
            for k in range(8):
                c = lanes(ra[k], sub + 8 * t)
                xa = xa - c * ra[k]
                xe = xe - c * re[k]
            tile[at, 0:128] = xa
            tile[at, 128:256] = xe


def eye(n):
    return (lax.broadcasted_iota(jnp.int32, (n, n), 0) == lax.broadcasted_iota(jnp.int32, (n, n), 1)).astype(f32)


def factor(mat, tile, cols):
    n = 128
    for lo in range(0, RANK, n):
        hi = lo + n
        tile[:, 0:n] = mat[lo:hi, lo:hi]
        tile[:, n : 2 * n] = eye(n)
        for part in range(4):
            factor128(tile, cols, range(4 * part, 4 * part + 4))
            yield
        mat[lo:hi, lo:hi] = eye(n)
        mat[lo:hi, :] = dot(tile[:, n : 2 * n], mat[lo:hi, :], precision=HIGHEST)
        if hi < RANK:
            mat[hi:, lo:hi] = jnp.zeros((RANK - hi, n), f32)
            mat[hi:, :] = mat[hi:, :] - dot(mat[lo:hi, hi:], mat[lo:hi, :], ((0,), (0,)), HIGHEST)
        yield


class Copies:
    def __init__(self, send, recv):
        self.send, self.recv = send, recv
        self.free, self.fresh, self.n, self.all, self.drained = [], 0, 0, [], 0

    def semaphore(self):
        self.n += 1
        return self.recv.at[self.n - 1]

    def new(self, src, dst, device, recv=None):
        if self.free:
            i = self.free.pop(0)
        else:
            i = self.fresh
            self.fresh += 1
        copy = pltpu.make_async_remote_copy(
            src_ref=src,
            dst_ref=dst,
            send_sem=self.send.at[i],
            recv_sem=self.semaphore() if recv is None else recv,
            device_id=device,
            device_id_type=MESH,
        )
        copy.start()
        self.all.append((copy, i))
        return copy

    def drain(self, upto):
        for copy, i in self.all[self.drained : upto]:
            copy.wait_send()
            self.free.append(i)
        self.drained = upto

    def count(self):
        return len(self.all)


def arrive(ref, semaphore):
    pltpu.make_async_copy(ref, ref, semaphore).wait()


class Ring:
    def __init__(self, copies, pos, right, left):
        self.copies, self.pos, self.right, self.left = copies, pos, right, left

    def place(self, base, size):
        first = (size // 2 + 7) // 8 * 8

        def at(step, part):
            offset = base + lax.rem(self.pos + step, 4) * size + part * first
            return pl.ds(pl.multiple_of(offset, 8), size - first if part else first)

        return at

    def reduce_start(self, ref, base, size, slots):
        new = self.copies.new
        at = self.place(base, size)
        self.ref, self.at = ref, at
        self.slots = [slots.at[i, 0 : at(0, 1 if i in (1, 3, 5) else 0).size] for i in range(6)]
        self.r = [None] * 6
        self.rest, self.whole = self.copies.semaphore(), slots.at[0:4]
        self.r[0] = new(ref.at[at(2, 0)], self.slots[0], self.right)
        self.r[3] = new(ref.at[at(2, 1)], self.slots[3], self.left)

    def reduce_plain(self):
        new, ref, at = self.copies.new, self.ref, self.at
        self.r[1] = new(ref.at[at(1, 1)], self.slots[1], self.right, self.rest)
        self.r[4] = new(ref.at[at(3, 0)], self.slots[4], self.left, self.rest)

    def reduce_middle(self):
        new, ref, slots = self.copies.new, self.ref, self.slots
        one, two = self.at(1, 0), self.at(3, 1)
        self.r[0].wait_recv()
        ref[one, :] = ref[one, :] + slots[0][...]
        self.r[2] = new(ref.at[one], slots[2], self.right, self.rest)
        self.r[3].wait_recv()
        ref[two, :] = ref[two, :] + slots[3][...]
        self.r[5] = new(ref.at[two], slots[5], self.left, self.rest)

    def reduce_end(self, out):
        ref, slots = self.ref, self.slots
        one, two = self.at(0, 0), self.at(0, 1)
        arrive(self.whole, self.rest)
        out[one, :] = ref[one, :] + slots[4][...] + slots[2][...]
        out[two, :] = ref[two, :] + slots[1][...] + slots[5][...]

    def gather_start(self, ref, base, size):
        new = self.copies.new
        at = self.place(base, size)
        self.out, self.gat = ref, at
        one, two = ref.at[at(0, 0)], ref.at[at(0, 1)]
        self.g = [None] * 6
        self.grest, self.gwhole = self.copies.semaphore(), ref.at[pl.ds(base, 2 * size)]
        self.g[0] = new(one, one, self.right)
        self.g[2] = new(two, two, self.left)

    def gather_rest(self):
        new, ref, at = self.copies.new, self.out, self.gat
        one, two = ref.at[at(0, 0)], ref.at[at(0, 1)]
        self.g[1] = new(two, two, self.right, self.grest)
        self.g[3] = new(one, one, self.left, self.grest)

    def gather_middle(self):
        new, ref, at = self.copies.new, self.out, self.gat
        one, two = ref.at[at(3, 0)], ref.at[at(1, 1)]
        self.g[0].wait_recv()
        self.g[4] = new(one, one, self.right, self.grest)
        self.g[2].wait_recv()
        self.g[5] = new(two, two, self.left, self.grest)

    def gather_end(self):
        arrive(self.gwhole, self.grest)


class Direct:
    def __init__(self, copies, pos, dev):
        self.copies, self.pos, self.dev = copies, pos, dev

    def group(self, step):
        return pl.ds(pl.multiple_of(self.base + lax.rem(self.pos + step, 4) * self.size, 8), self.size)

    def reduce_start(self, ref, base, size, slots):
        self.ref, self.base, self.size, self.slots = ref, base, size, slots
        self.sem = self.copies.semaphore()
        for i in (2, 1, 3):
            self.copies.new(ref.at[self.group(i)], slots.at[i - 1], self.dev(i), self.sem)

    def reduce_end(self, out):
        arrive(self.slots, self.sem)
        at = self.group(0)
        out[at, :] = (self.ref[at, :] + self.slots[0]) + (self.slots[1] + self.slots[2])

    def gather_start(self, ref):
        own = ref.at[self.group(0)]
        self.sem = self.copies.semaphore()
        for i in (2, 1, 3):
            self.copies.new(own, own, self.dev(i), self.sem)

    def gather_end(self):
        arrive(self.slots, self.sem)


def dion_kernel(
    grad_hbm, mom_hbm, basis_hbm,
    nm_ref, nb_ref, uh, ul, inv_ref,
    grad, mom, bh, bl, qh, ql,
    pacc, pother, pown, precv, pslots, pfull, ph, plo,
    prow, gpart, gsum, gslots1, gslots2, gslots3, gmat, mat, tile, cols,
    zpart, zslots1, zslots2, zfull, lh, ll, squares, sqslots,
    load_sem, send_sem, recv_sem,
):
    f, t = lax.axis_index("fsdp"), lax.axis_index("tp")
    z, x, y, c = f // 4, f % 4, t // 2, t % 2

    def zdev(step):
        return (lax.rem(z + step, 4) * 4 + x, t)

    def xdev(step):
        return (z * 4 + lax.rem(x + step, 4), t)

    def ydev(step):
        return (f, lax.rem(y + step, 4) * 2 + c)

    def tdev(step):
        return (f, lax.rem(t + step, 8))

    sibling = (f, y * 2 + 1 - c)

    barrier = pltpu.get_barrier_semaphore()
    peers = [zdev(i) for i in (1, 2, 3)] + [xdev(i) for i in (1, 2, 3)] + [tdev(i) for i in range(1, 8)]
    for peer in peers:
        pl.semaphore_signal(barrier, inc=1, device_id=peer, device_id_type=MESH)

    def load(k):
        at = pl.ds(k * CHUNK, CHUNK)
        pltpu.make_async_copy(mom_hbm.at[:, at], mom.at[:, at], load_sem.at[k]).start()
        pltpu.make_async_copy(grad_hbm.at[:, at], grad.at[:, at], load_sem.at[k]).start()
        for half in range(2):
            pltpu.make_async_copy(
                basis_hbm.at[at, pl.ds(half * HALF, HALF)], zfull.at[half, at], load_sem.at[k]
            ).start()

    for k in range(CHUNKS):
        load(k)
    loaded = zpart.at[0, 0:1280]

    copies = Copies(send_sem, recv_sem)

    def partial(q, k):
        at = slice(k * CHUNK, k * CHUNK + CHUNK)
        columns = slice(q * HALF, q * HALF + HALF)
        term = dot3((bh[:, at], bl[:, at]), (qh[at, columns], ql[at, columns]))
        pacc[q] = term if k == 0 else pacc[q] + term

    def swap_start(q):
        pother[q] = pacc[q, :, pl.ds(pl.multiple_of((1 - c) * 128, 128), 128)]
        return copies.new(pother.at[q], precv.at[q], sibling)

    yring = [Ring(copies, y, ydev(1), ydev(3)) for _ in range(2)]

    def yrs_start(q):
        swaps[q].wait_recv()
        pown[q] = pacc[q, :, pl.ds(pl.multiple_of(c * 128, 128), 128)] + precv[q]
        yring[q].reduce_start(pown.at[q], 0, 128, pslots.at[q])
        yring[q].reduce_plain()

    shared = [[copies.semaphore() for _ in range(2)] for _ in range(2)]

    def share(q, step, semaphore):
        part = pfull.at[q, c, pl.ds(pl.multiple_of(lax.rem(y + step, 4) * 128, 128), 128)]
        copies.new(part, part, sibling, semaphore)

    def yrs_end(q):
        yring[q].reduce_end(pfull.at[q, c])
        yring[q].gather_start(pfull.at[q, c], 0, 128)
        yring[q].gather_rest()
        share(q, 0, shared[q][0])

    def yag_end(q):
        yring[q].gather_end()
        for step in (1, 2, 3):
            share(q, step, shared[q][1])

    for k in range(CHUNKS):
        at = slice(k * CHUNK, k * CHUNK + CHUNK)
        arrive(loaded, load_sem.at[k])
        bh[:, at], bl[:, at] = split(mom[:, at] + grad[:, at].astype(f32))
        for half in range(2):
            columns = slice(half * HALF, half * HALF + HALF)
            qh[at, columns], ql[at, columns] = split(zfull[half, at, :])
        partial(0, k)
    pl.semaphore_wait(barrier, len(peers))
    swaps = [swap_start(0)]
    for k in range(CHUNKS):
        partial(1, k)
    swaps.append(swap_start(1))
    yrs_start(0)
    yrs_start(1)
    yring[0].reduce_middle()
    yring[1].reduce_middle()
    yrs_end(0)
    yrs_end(1)

    own_rows = pl.ds(pl.multiple_of(y * 128, 128), 128)
    for q in range(2):
        arrive(precv.at[q, 0:128], shared[q][0])
        for j in range(2):
            prow[:, q * HALF + j * 128 : q * HALF + j * 128 + 128] = pfull[q, j, own_rows, :]
    block = lambda i, width=1: prow[:, pl.ds(pl.multiple_of(i * 128, 128), width * 128)]
    over = ((0,), (0,))
    gpart[:, 0:384] = dot(block(c), block(c, 3), over, HIGHEST)
    gpart[:, 384:512] = dot(block(2 * c), block(3 - c), over, HIGHEST)
    gpart[:, 512:640] = dot(block(3 - c), block(3), over, HIGHEST)
    parts = (pl.ds(0, 384), pl.ds(384, 256))
    axes = ((z, zdev), (x, xdev))

    def rows(pos, step, size, base=0):
        return pl.ds(pl.multiple_of(base + lax.rem(pos + step, 4) * size, 8), size)

    def gram_send(stage):
        semaphore = copies.semaphore()
        for step in (1, 2, 3):
            for g in range(2):
                (pos, dev), (pos2, dev2) = axes[g], axes[1 - g]
                if stage == 1:
                    src, dst, to = gpart.at[rows(pos, step, 32), parts[g]], gslots1.at[step - 1, :, parts[g]], dev(step)
                elif stage == 2:
                    at = rows(pos2, step, 8, pos * 32)
                    src, dst, to = gsum.at[at, parts[g]], gslots2.at[step - 1, :, parts[g]], dev2(step)
                elif stage == 3:
                    at = rows(pos2, 0, 8, pos * 32)
                    src, dst, to = gsum.at[at, parts[g]], gslots3.at[step - 1, :, parts[g]], ydev(step)
                elif stage == 4:
                    at = rows(pos2, 0, 8, pos * 32)
                    src, dst, to = gmat.at[c, at, parts[g]], gmat.at[c, at, parts[g]], dev2(step)
                else:
                    at = rows(pos, 0, 32)
                    src, dst, to = gmat.at[c, at, parts[g]], gmat.at[c, at, parts[g]], dev(step)
                copies.new(src, dst, to, semaphore)
        return semaphore

    def gram_wait(stage, sent):
        arrive({1: gslots1, 2: gslots2, 3: gslots3, 4: gslots3, 5: gslots1}[stage], sent)
        if stage > 3:
            return
        for g in range(2):
            pos, pos2 = axes[g][0], axes[1 - g][0]
            if stage == 1:
                at = rows(pos, 0, 32)
                own, slots, out = gpart[at, parts[g]], gslots1, gsum
            elif stage == 2:
                at = rows(pos2, 0, 8, pos * 32)
                own, slots, out = gsum[at, parts[g]], gslots2, gsum
            else:
                at = rows(pos2, 0, 8, pos * 32)
                own, slots, out = gsum[at, parts[g]], gslots3, gmat.at[c]
            out[at, parts[g]] = (own + slots[0, :, parts[g]]) + (slots[1, :, parts[g]] + slots[2, :, parts[g]])

    sent = gram_send(1)
    yring[0].gather_middle()
    yring[1].gather_middle()
    yag_end(0)

    def product(q):
        arrive(precv.at[q, 0:384], shared[q][1])
        for j in range(2):
            ph[q, :, j * 128 : j * 128 + 128], plo[q, :, j * 128 : j * 128 + 128] = split(pfull[q, j])
        for k in range(CHUNKS):
            at = slice(k * CHUNK, k * CHUNK + CHUNK)
            zpart[q, at, :] = dot3((bh[:, at], bl[:, at]), (ph[q], plo[q]), ((0,), (0,)))

    tall = COL // 8
    short = tall // 4
    starts = (0, COL // 2)
    bases = (z * tall, COL // 2 + x * tall)
    first = [[Ring(copies, z, zdev(1), zdev(3)), Ring(copies, x, xdev(1), xdev(3))] for _ in range(2)]
    second = [[Direct(copies, x, xdev), Direct(copies, z, zdev)] for _ in range(2)]

    def rs1_start(q):
        for g in range(2):
            first[q][g].reduce_start(zpart.at[q], starts[g], tall, zslots1.at[q, g])
        for g in range(2):
            first[q][g].reduce_plain()

    def rs1_middle(q):
        for g in range(2):
            first[q][g].reduce_middle()

    def rs1_end(q):
        for g in range(2):
            first[q][g].reduce_end(zpart.at[q])
            second[q][g].reduce_start(zpart.at[q], bases[g], short, zslots2.at[q, g])

    def rs2_end(q):
        for g in range(2):
            second[q][g].reduce_end(zfull.at[q])
            second[q][g].gather_start(zfull.at[q])

    def ag1_end(q):
        for g in range(2):
            second[q][g].gather_end()
            first[q][g].gather_start(zfull.at[q], starts[g], tall)

    def ag2_rest(q):
        for g in range(2):
            first[q][g].gather_rest()

    def ag2_middle(q):
        for g in range(2):
            first[q][g].gather_middle()

    def ag2_end(q):
        for g in range(2):
            first[q][g].gather_end()

    gram_wait(1, sent)
    sent = gram_send(2)
    product(0)
    gram_wait(2, sent)
    sent = gram_send(3)
    rs1_start(0)
    sums_sent = copies.count()
    yag_end(1)
    product(1)
    copies.drain(sums_sent - 20)
    gram_wait(3, sent)
    sent = gram_send(4)
    rs1_middle(0)
    gram_wait(4, sent)
    sent = gram_send(5)
    rs1_start(1)
    first_sent = copies.count()
    rs1_end(0)
    gram_wait(5, sent)
    swap = copies.new(gmat.at[c], gmat.at[c], sibling)
    swap.wait_recv()
    for i, g, first_block, width, where in (
        (0, 0, 0, 3, 0), (0, 0, 3, 1, 384), (3, 0, 3, 1, 512),
        (1, 1, 1, 3, 0), (2, 1, 2, 1, 384), (2, 1, 3, 1, 512),
    ):
        mat[i * 128 : i * 128 + 128, first_block * 128 : (first_block + width) * 128] = gmat[
            g, :, where : where + width * 128
        ]

    work = factor(mat, tile, cols)

    def steps(n):
        for _ in range(n):
            next(work)

    steps(2)
    rs1_middle(1)
    steps(4)
    rs2_end(0)
    steps(3)
    rs1_end(1)
    steps(2)
    ag1_end(0)
    steps(3)
    rs2_end(1)
    ag2_rest(0)
    copies.drain(first_sent)
    steps(4)
    ag2_middle(0)
    steps(2)
    r = lax.broadcasted_iota(jnp.int32, (RANK, RANK), 0)
    k = lax.broadcasted_iota(jnp.int32, (RANK, RANK), 1)
    lh[...], ll[...] = split(jnp.where(r >= k, mat[...], 0.0))
    last = ((1,), (1,))

    def solve(pairs):
        low, high = slice(0, HALF), slice(HALF, RANK)
        factor_of = lambda rows_, columns: (lh[rows_, columns], ll[rows_, columns])
        left = dot3(pairs[0], factor_of(low, low), last)
        right = dot3(pairs[0], factor_of(high, low), last) + dot3(pairs[1], factor_of(high, high), last)
        return left, right

    shard = [
        jnp.concatenate([zfull[q, second[q][g].group(0), :] for g in range(2)], axis=0) for q in range(2)
    ]
    for q, w in enumerate(solve([split(part) for part in shard])):
        squares[0, :, q * HALF : q * HALF + HALF] = jnp.sum((w * w).reshape(short // 4, 8, HALF), axis=0)

    def norm_send(stage):
        steps_, dev = ((1, 2, 3), zdev) if stage == 0 else ((1, 2, 3), xdev) if stage == 1 else (range(1, 8), tdev)
        semaphore = copies.semaphore()
        for i in steps_:
            copies.new(squares.at[stage], sqslots.at[stage, i - 1], dev(i), semaphore)
        return semaphore

    def norm_wait(stage, sent):
        total = squares[stage]
        number = 7 if stage == 2 else 3
        arrive(sqslots.at[stage, 0:number], sent)
        for i in range(number):
            total = total + sqslots[stage, i]
        squares[stage + 1] = total

    sent = norm_send(0)
    ag1_end(1)
    ag2_rest(1)
    for q, u in enumerate(solve([(ph[half], plo[half]) for half in range(2)])):
        at = slice(q * HALF, q * HALF + HALF)
        uh[:, at], ul[:, at] = split(u)

    low, high = slice(0, HALF), slice(HALF, RANK)

    def early(k):
        at = slice(k * CHUNK, k * CHUNK + CHUNK)
        part = split(zfull[0, at, :])
        nb_ref[at, low] = dot3(part, (lh[low, low], ll[low, low]), last)
        nb_ref[at, high] = dot3(part, (lh[high, low], ll[high, low]), last)

    def back(k):
        at = slice(k * CHUNK, k * CHUNK + CHUNK)
        nb_ref[at, high] = nb_ref[at, high] + dot3(split(zfull[1, at, :]), (lh[high, high], ll[high, high]), last)
        update = dot(uh[...], nb_ref[at, :].astype(bf16), last)
        nm_ref[:, at] = (mom[:, at] + grad[:, at].astype(f32)) - 0.05 * update

    most_sent = copies.count() - 16
    norm_wait(0, sent)
    sent = norm_send(1)
    ag2_end(0)
    for i in range(3):
        early(i)
    ag2_middle(1)
    norm_wait(1, sent)
    sent = norm_send(2)
    for i in range(3, CHUNKS):
        early(i)
    copies.drain(most_sent)
    ag2_end(1)
    for i in range(CHUNKS):
        back(i)
    norm_wait(2, sent)
    norms = jnp.sqrt(jnp.sum(squares[3], axis=0, keepdims=True))
    inv_ref[...] = jnp.broadcast_to(1.0 / (norms + 1e-08), (8, RANK))
    copies.drain(copies.count())


def finish_kernel(scale, nm, w, uh, ul, inv, nm_out, nb_out, up_out, nb, up, sem):
    pltpu.make_async_copy(nm, nm_out, sem.at[0]).start()
    for k in range(CHUNKS):
        at = slice(k * CHUNK, k * CHUNK + CHUNK)
        n = w[at, :] * inv[0:1, :]
        nb[at, :] = n
        pltpu.make_async_copy(nb.at[at, :], nb_out.at[at, :], sem.at[1]).start()
        up[:, at] = (scale * dot3((uh[...], ul[...]), split(n), ((1,), (1,)))).astype(bf16)
        pltpu.make_async_copy(up.at[:, at], up_out.at[:, at], sem.at[2]).start()
    for i, (src, dst) in enumerate(((nm, nm_out), (nb, nb_out), (up, up_out))):
        pltpu.make_async_copy(src, dst, sem.at[i]).wait()


SENDS = 84
ARRIVALS = 59


def local(gradient, momentum, basis):
    vmem = lambda shape, kind=f32: pltpu.VMEM(shape, kind)
    shapes = [
        jax.ShapeDtypeStruct((ROW, COL), f32),
        jax.ShapeDtypeStruct((COL, RANK), f32),
        jax.ShapeDtypeStruct((ROW, COL), bf16),
    ]
    results = pl.pallas_call(
        dion_kernel,
        out_shape=shapes[:2] + [
            jax.ShapeDtypeStruct((ROW, RANK), bf16),
            jax.ShapeDtypeStruct((ROW, RANK), bf16),
            jax.ShapeDtypeStruct((8, RANK), f32),
        ],
        in_specs=[pl.BlockSpec(memory_space=pltpu.HBM)] * 3,
        out_specs=[pl.BlockSpec(memory_space=pltpu.VMEM)] * 5,
        scratch_shapes=[
            vmem((ROW, COL), bf16), vmem((ROW, COL)),
            vmem((ROW, COL), bf16), vmem((ROW, COL), bf16),
            vmem((COL, RANK), bf16), vmem((COL, RANK), bf16),
            vmem((2, ROW, HALF)), vmem((2, ROW, 128)), vmem((2, ROW, 128)), vmem((2, ROW, 128)),
            vmem((2, 6, 64, 128)), vmem((2, 2, ROW, 128)),
            vmem((2, ROW, HALF), bf16), vmem((2, ROW, HALF), bf16),
            vmem((128, RANK)), vmem((128, 640)), vmem((128, 640)),
            vmem((3, 32, 640)), vmem((3, 8, 640)), vmem((3, 8, 640)), vmem((2, 128, 640)), vmem((RANK, RANK)),
            vmem((128, 256)), vmem((64, 128)),
            vmem((2, COL, HALF)), vmem((2, 2, 6, COL // 16, HALF)), vmem((2, 2, 3, COL // 32, HALF)),
            vmem((2, COL, HALF)),
            vmem((RANK, RANK), bf16), vmem((RANK, RANK), bf16),
            vmem((4, 8, RANK)), vmem((3, 7, 8, RANK)),
            pltpu.SemaphoreType.DMA((CHUNKS,)),
            pltpu.SemaphoreType.DMA((SENDS,)),
            pltpu.SemaphoreType.DMA((ARRIVALS,)),
        ],
        compiler_params=pltpu.CompilerParams(
            collective_id=0, has_side_effects=True, vmem_limit_bytes=40 << 20
        ),
        name="dion",
    )(*(pltpu.with_memory_space_constraint(a, pltpu.HBM) for a in (gradient, momentum, basis)))
    return tuple(pl.pallas_call(
        functools.partial(finish_kernel, float((ROWS * COLS / RANK) ** 0.5)),
        out_shape=shapes,
        in_specs=[pl.BlockSpec(memory_space=pltpu.VMEM)] * 5,
        out_specs=[pl.BlockSpec(memory_space=pltpu.HBM)] * 3,
        scratch_shapes=[vmem((COL, RANK)), vmem((ROW, COL), bf16), pltpu.SemaphoreType.DMA((3,))],
        compiler_params=pltpu.CompilerParams(vmem_limit_bytes=10 << 20),
        name="finish",
    )(*results))


def solution(mesh):
    return jax.shard_map(
        local,
        mesh=mesh,
        in_specs=(P("fsdp", "tp"), P("fsdp", "tp"), P("tp", None)),
        out_specs=(P("fsdp", "tp"), P("tp", None), P("fsdp", "tp")),
        check_vma=False,
    )
```
